32 devices in a mesh: seq: 4 (over x, core), dp: 8 (over z, y).
Axes of the slice: x: 2, y: 2, z: 4, core: 2. Of those that a mesh axis runs over, the one named last changes fastest.
Arguments:
- tokens: bfloat16 [8, 1024, 2048], P('dp', 'seq'), may hold values from -6 to 6
- joint_weight: bfloat16 [2048, 6144], P(('seq', 'dp')), may hold values from -0.125 to 0.125
- output_weight: bfloat16 [2048, 2048], P(('seq', 'dp')), may hold values from -0.5 to 0.5
- up_weight: bfloat16 [2048, 8192], P(('seq', 'dp')), may hold values from -0.125 to 0.125
- down_weight: bfloat16 [2048, 8192], P(('seq', 'dp')), may hold values from -0.0625 to 0.0625
- joint_bias: bfloat16 [6144], P(('seq', 'dp')), may hold values from -1.1953125 to 1.1953125
- output_bias: bfloat16 [2048], P(('seq', 'dp')), may hold values from -1.1953125 to 1.1953125
- up_bias: bfloat16 [8192], P(('seq', 'dp')), may hold values from -1.1953125 to 1.1953125
- down_bias: bfloat16 [2048], P(('seq', 'dp')), may hold values from -1.1953125 to 1.1953125
- norm_gain: bfloat16 [2048], P(('seq', 'dp')), may hold values from 0.5 to 1.5
- norm_shift: bfloat16 [2048], P(('seq', 'dp')), may hold values from -1.1953125 to 1.1953125
- segments: int32 [8, 1024], P('dp', 'seq'), may hold values from 0 to 2, as said below
- positions: int32 [8, 1024], P('dp', 'seq'), may hold values from 0 to 895, as said below
- cotangent: bfloat16 [8, 1024, 2048], P('dp', 'seq'), may hold values from -6 to 6
Outputs:
- layer_out: bfloat16 [8, 1024, 2048], P('dp', 'seq')
- tokens_grad: bfloat16 [8, 1024, 2048], P('dp', 'seq')
- joint_weight_grad: float32 [2048, 6144], P(('seq', 'dp'))
- output_weight_grad: float32 [2048, 2048], P(('seq', 'dp'))
- up_weight_grad: float32 [2048, 8192], P(('seq', 'dp'))
- down_weight_grad: float32 [2048, 8192], P(('seq', 'dp'))
- joint_bias_grad: float32 [6144], P(('seq', 'dp'))
- output_bias_grad: float32 [2048], P(('seq', 'dp'))
- up_bias_grad: float32 [8192], P(('seq', 'dp'))
- down_bias_grad: float32 [2048], P(('seq', 'dp'))
- norm_gain_grad: float32 [2048], P(('seq', 'dp'))
- norm_shift_grad: float32 [2048], P(('seq', 'dp'))
The draws below stay inside these ranges and needn't reach their ends.
Inputs may be any that keep to these rules, and one draw needn't show every extreme that they name: `segments`: in each sequence the segment numbers never fall and each of 0, 1, 2 occurs; documents 0 and 2 hold fewer than 128 tokens each, at least one. `positions`: A token's place within its document, counting from 0 at the document's first token; document 1 of every sequence holds exactly 1024 - max(2, 128) tokens.
All inputs are finite; a program needn't handle non-finite values.
Results may differ from the reference program's by a relative error of at most 0.0079.
Values may be sent and summed in bfloat16 or wider, within the bound.
No kernel may reach another device: no remote copies, remote signals or barrier semaphores. Data moves between devices by JAX's collectives and lax.ppermute only.
A program may use at most 704 MiB of HBM per device.

```python
import jax
import jax.numpy as jnp
from jax import lax

D = 2048
H = 32
HD = 64
ROT = 32
FF = 8192
TOK_DEV = 256
SEQ_LEN = 1024
SEQS = 8


def document_bounds(key):
    margin = max(2, TOK_DEV // 2)
    opening = jax.random.randint(key, (SEQS, 1), 1, margin)
    closing = opening + (SEQ_LEN - margin)
    return (opening, closing)


def draw_segments(key, part):
    opening, closing = document_bounds(key)
    places = jnp.arange(SEQ_LEN, dtype=jnp.int32)[None, :]
    return (places >= opening).astype(jnp.int32) + (places >= closing).astype(jnp.int32)


def draw_positions(key, part):
    opening, closing = document_bounds(key)
    places = jnp.arange(SEQ_LEN, dtype=jnp.int32)[None, :]
    inside = jnp.where(places >= opening, places - opening, places)
    return jnp.where(places >= closing, places - closing, inside).astype(jnp.int32)


def shard_levels(stream_key, shape, pieces, low, top_value):
    def one(position, blocks):
        heights = jax.random.uniform(jax.random.fold_in(jax.random.fold_in(stream_key, 6), position), (blocks,), jnp.float32, low / len(pieces), top_value / len(pieces))
        return jnp.repeat(jnp.exp(heights), shape[position] // blocks).reshape((-1,) + (1,) * (len(shape) - position - 1))

    factor_of = one(*pieces[0])
    for cut in pieces[1:]:
        factor_of = factor_of * one(*cut)
    return factor_of


def scatter_about(rng, shape, spread, reach, pieces=(), kind=jnp.bfloat16):
    values = jax.random.normal(rng, shape, jnp.float32) * spread
    if len(pieces) > 0:
        values = shard_levels(rng, shape, pieces, -0.22, 0.18) * values
    return jnp.clip(values, min=-reach, max=reach).astype(kind)


def setup_inputs(seed: int = 0) -> dict:
    key_of = jax.random.split(jax.random.key(seed), 15)
    tokens = scatter_about(key_of[0], (SEQS, SEQ_LEN, D), 1.0, 6.0, ((0, 8), (1, 4)))
    joint_weight = scatter_about(key_of[1], (D, 3 * D), D ** -0.5, 0.125, ((0, 32),))
    output_weight = scatter_about(key_of[2], (D, D), (D // 16) ** -0.5, 0.5, ((0, 32),))
    up_weight = scatter_about(key_of[3], (D, FF), D ** -0.5, 0.125, ((0, 32),))
    down_weight = scatter_about(key_of[4], (D, FF), FF ** -0.5, 0.0625, ((0, 32),))
    joint_bias = scatter_about(key_of[5], (3 * D,), 0.2, 1.1953125, ((0, 32),))
    output_bias = scatter_about(key_of[6], (D,), 0.2, 1.1953125, ((0, 32),))
    up_bias = scatter_about(key_of[7], (FF,), 0.2, 1.1953125, ((0, 32),))
    down_bias = scatter_about(key_of[8], (D,), 0.2, 1.1953125, ((0, 32),))
    norm_gain = jnp.clip(1.0 + 0.1 * jax.random.normal(key_of[9], (D,), jnp.float32), 0.5, 1.5).astype(jnp.bfloat16)
    norm_shift = scatter_about(key_of[10], (D,), 0.2, 1.1953125, ((0, 32),))
    segments = draw_segments(jax.random.fold_in(key_of[14], 71), 0)
    positions = draw_positions(jax.random.fold_in(key_of[14], 71), 0)
    cotangent = scatter_about(key_of[13], (SEQS, SEQ_LEN, D), 1.0, 6.0, ((0, 8), (1, 4)))
    return dict(tokens=tokens, joint_weight=joint_weight, output_weight=output_weight, up_weight=up_weight, down_weight=down_weight, joint_bias=joint_bias, output_bias=output_bias, up_bias=up_bias, down_bias=down_bias, norm_gain=norm_gain, norm_shift=norm_shift, segments=segments, positions=positions, cotangent=cotangent)


NEG_FILL = -1e+30
NORM_EPS = 1e-05
HIGHEST = lax.Precision.HIGHEST

@jax.custom_vjp
def low(v):
    return lax.optimization_barrier(v.astype(jnp.bfloat16)).astype(jnp.float32)

@jax.custom_vjp
def low_back(v):
    return v

def low_keep(v):
    return (low(v), None)

def low_pass(kept, grad):
    return (grad,)

def back_keep(v):
    return (v, None)

def back_low(kept, grad):
    return (low(grad),)
low.defvjp(low_keep, low_pass)
low_back.defvjp(back_keep, back_low)

def turn_tables(places):
    frequency = 10000.0 ** (-jnp.arange(0, ROT, 2, dtype=jnp.float32) / ROT)
    angles = places.astype(jnp.float32)[:, None] * frequency[None, :]
    angles = jnp.concatenate([angles, angles], 1)
    return (jnp.cos(angles)[:, None, :], jnp.sin(angles)[:, None, :])

def rotate(inputs, cosine_table, sine_table):
    half_rot = ROT // 2
    rotary = inputs[..., :ROT]
    turned = jnp.concatenate([-rotary[..., half_rot:], rotary[..., :half_rot]], -1)
    return jnp.concatenate([rotary * cosine_table + turned * sine_table, inputs[..., ROT:]], -1)

def one_sequence(params, inputs, documents, places):
    joint_weight, output_weight, up_weight, down_weight, joint_bias, output_bias, up_bias, down_bias, norm_gain, norm_shift = params
    length = inputs.shape[0]
    centered = inputs - lax.optimization_barrier(jnp.mean(inputs, 1, keepdims=True))
    normed = low(centered * lax.rsqrt(lax.optimization_barrier(jnp.mean(centered * centered, 1, keepdims=True)) + NORM_EPS) * norm_gain + norm_shift)
    joint_out = low_back(jnp.dot(normed, joint_weight, precision=HIGHEST) + joint_bias)
    cosine_table, sine_table = turn_tables(places)
    queries = low(rotate(joint_out[:, :D].reshape(length, H, HD), cosine_table, sine_table))
    key_low = low(rotate(joint_out[:, D:2 * D].reshape(length, H, HD), cosine_table, sine_table))
    values = low(joint_out[:, 2 * D:].reshape(length, H, HD))
    scores = low_back(HD ** (-0.5) * jnp.einsum('qhd,khd->hqk', queries, key_low, precision=HIGHEST))
    indices = jnp.arange(length)
    allowed = (documents[:, None] == documents[None, :]) & (indices[None, :] <= indices[:, None])
    softmaxed = low(jax.nn.softmax(jnp.where(allowed[None], scores, NEG_FILL), axis=-1))
    attended = jnp.einsum('hqk,khd->qhd', softmaxed, values, precision=HIGHEST).reshape(length, D)
    attended = low_back(low(attended))
    branch = jnp.dot(attended, output_weight, precision=HIGHEST) + output_bias
    up_pre = low_back(jnp.dot(normed, up_weight, precision=HIGHEST) + up_bias)
    hidden = low(jax.nn.gelu(up_pre, approximate=True))
    feed_out = jnp.dot(hidden, down_weight.T, precision=HIGHEST) + down_bias
    return inputs + branch + feed_out

def reference(tokens, joint_weight, output_weight, up_weight, down_weight, joint_bias, output_bias, up_bias, down_bias, norm_gain, norm_shift, segments, positions, cotangent):
    params = tuple((weight.astype(jnp.float32) for weight in (joint_weight, output_weight, up_weight, down_weight, joint_bias, output_bias, up_bias, down_bias, norm_gain, norm_shift)))
    checked = jax.checkpoint(one_sequence)

    def forward(params, inputs):

        def advance(unused, sequence):
            return (unused, checked(params, sequence[0], sequence[1], sequence[2]))
        return lax.scan(advance, None, (inputs, segments, positions))[1]
    outputs, pullback = jax.vjp(forward, params, tokens.astype(jnp.float32))
    param_grads, input_grads = pullback(cotangent.astype(jnp.float32))
    return (outputs.astype(jnp.bfloat16), input_grads.astype(jnp.bfloat16), param_grads[0], param_grads[1], param_grads[2], param_grads[3], param_grads[4], param_grads[5], param_grads[6], param_grads[7], param_grads[8], param_grads[9])
```

```python
import functools

import jax
import jax.numpy as jnp
from jax import lax
from jax.experimental import pallas as pl
from jax.experimental.pallas import tpu as pltpu
from jax.sharding import Mesh
from jax.sharding import PartitionSpec as P

ALL = ("x", "c", "zh", "zl", "y")
H = 32
HD = 64
ROT = 32
PAIR = 2 * HD
NEG_FILL = -1e30
NORM_EPS = 1e-05
F32 = jnp.float32
BF16 = jnp.bfloat16


def dot(left, right, left_dim, right_dim):
    return lax.dot_general(
        left, right, (((left_dim,), (right_dim,)), ((), ())), preferred_element_type=F32
    )


def swap(value, axis):
    return lax.ppermute(value, axis, [(0, 1), (1, 0)])


def in_order(own, other, place, dim):
    return jnp.where(
        place == 0, jnp.stack([own, other], dim), jnp.stack([other, own], dim)
    )


def pick(value, place, dim):
    return lax.dynamic_index_in_dim(value, place, dim, keepdims=False)


def exchange(value, axes_dims):
    for axis, dim in axes_dims:
        place = lax.axis_index(axis)
        other = swap(pick(value, 1 - place, dim), axis)
        value = in_order(pick(value, place, dim), other, place, dim)
    return value


TEAM = (("c", 1), ("x", 0), ("zl", 2))


def team_gather(value):
    value = jnp.stack([value, swap(value, "zl")])
    value = jnp.stack([value, swap(value, "x")])
    return jnp.stack([value, swap(value, "c")])


def team_sum(value):
    for axis in ("c", "x", "zl"):
        other = swap(value[1].astype(BF16), axis)
        value = value[0].astype(F32) + other.astype(F32)
    return value


def rows_gather(value, mesh):
    place = lax.axis_index("zh")
    value = in_order(value, swap(value, "zh"), place, 2)
    if mesh.shape["y"] == 2:
        return in_order(value, swap(value, "y"), lax.axis_index("y"), 4)
    return lax.all_gather(value, "y", axis=4)


def rows_sum(value, mesh):
    if mesh.shape["y"] == 2:
        place = lax.axis_index("y")
        other = swap(pick(value, 1 - place, 4).astype(BF16), "y")
        value = pick(value, place, 4).astype(F32) + other.astype(F32)
    else:
        value = lax.psum_scatter(value.astype(BF16), "y", scatter_dimension=4).astype(F32)
    place = lax.axis_index("zh")
    other = swap(pick(value, 1 - place, 2).astype(BF16), "zh")
    return pick(value, place, 2).astype(F32) + other.astype(F32)


def turn(value, cosine, sine, lane, sign):
    half = ROT // 2
    width = value.shape[-1]
    up = pltpu.roll(value, width - half, 1)
    down = pltpu.roll(value, half, 1)
    turned = jnp.where(lane < half, -up, down)
    return value * cosine + (sign * turned) * sine


def attend_kernel(
    order, q_ref, k_ref, v_ref, do_ref, cos_ref, sin_ref, segc_ref, segr_ref,
    out_ref, grad_ref, qs, ks, vs, ds, kt, vt, segc, segr, dq, dk, dv,
):
    rows = q_ref.shape[2]
    blocks = q_ref.shape[0]
    pair = pl.program_id(1)
    scale = HD ** (-0.5)
    lane = lax.broadcasted_iota(jnp.int32, (rows, PAIR), 1) % HD

    def place(block):
        return pl.ds(pl.multiple_of(order[block] * rows, rows), rows)

    for block in range(blocks):
        at = place(block)
        cosine, sine = cos_ref[block, 0], sin_ref[block, 0]
        query = turn(q_ref[block, 0], cosine, sine, lane, 1.0).astype(BF16)
        qs[at, :] = query * jnp.asarray(scale, BF16)
        key = turn(k_ref[block, 0], cosine, sine, lane, 1.0)
        ks[at, :] = key.astype(BF16)
        kt[:, at] = key.T.astype(BF16)
        value = v_ref[block, 0]
        vs[at, :] = value.astype(BF16)
        vt[:, at] = value.T.astype(BF16)
        ds[at, :] = do_ref[block, 0]
        segc[at, :] = segc_ref[block, 0]
        segr[:, at] = segr_ref[block, 0]
    dk[...] = jnp.zeros_like(dk)
    dv[...] = jnp.zeros_like(dv)
    side = lax.broadcasted_iota(jnp.int32, (rows, PAIR), 1) // HD
    causal = lax.broadcasted_iota(jnp.int32, (rows, rows), 0) <= lax.broadcasted_iota(
        jnp.int32, (rows, rows), 1
    )
    for block in range(blocks):
        here = slice(block * rows, (block + 1) * rows)
        count = (block + 1) * rows
        same = segc[:count, :1] == segr[:1, here]
        if block == 0:
            allowed = same & causal
        else:
            allowed = jnp.concatenate([same[: count - rows], same[count - rows :] & causal], 0)
        query, grad = qs[here, :], ds[here, :]
        tops = []
        turns = []
        for head in range(2):
            lanes = slice(head * HD, (head + 1) * HD)
            query_one = jnp.where(side == head, query, jnp.zeros_like(query))
            grad_one = jnp.where(side == head, grad, jnp.zeros_like(grad))
            scores = dot(ks[:count, :], query_one, 1, 1)
            scores = jnp.where(allowed, scores, NEG_FILL)
            exps = jnp.exp(scores - jnp.max(scores, 0, keepdims=True))
            probs = exps * (1.0 / jnp.sum(exps, 0, keepdims=True))
            probs_low = probs.astype(BF16)
            tops.append(dot(vt[lanes, :count], probs_low, 1, 0))
            dv[:count, :] += dot(probs_low, grad_one, 1, 0)
            probs_grad = dot(vs[:count, :], grad_one, 1, 1)
            inner = jnp.sum(probs * probs_grad, 0, keepdims=True)
            score_grad = (probs * (probs_grad - inner)).astype(BF16)
            dk[:count, :] += dot(score_grad, query_one, 1, 0)
            turns.append(dot(kt[lanes, :count], score_grad, 1, 0))
        ds[here, :] = jnp.concatenate(tops, 0).T.astype(BF16)
        dq[here, :] = (jnp.concatenate(turns, 0) * scale).T
    for block in range(blocks):
        at = place(block)
        cosine, sine = cos_ref[block, 0], sin_ref[block, 0]
        out_ref[block, 0] = ds[at, :]
        for part, source in enumerate((dq, dk)):
            spot = pl.ds(pl.multiple_of(part * 2 * PAIR + pair * PAIR, PAIR), PAIR)
            grad_ref[block, 0, :, spot] = turn(source[at, :], cosine, sine, lane, -1.0).astype(BF16)
        spot = pl.ds(pl.multiple_of(4 * PAIR + pair * PAIR, PAIR), PAIR)
        grad_ref[block, 0, :, spot] = dv[at, :].astype(BF16)


def attend(order, joint, grad, cosine, sine, segc, segr):
    blocks, seqs, rows, width = joint.shape
    span = blocks * rows
    third = width // 3

    def part(first):
        return pl.BlockSpec((blocks, 1, rows, PAIR), lambda s, p, o: (0, s, 0, first + p))

    def table(height, wide):
        return pl.BlockSpec((blocks, 1, height, wide), lambda s, p, o: (0, s, 0, 0))

    return pl.pallas_call(
        attend_kernel,
        grid_spec=pltpu.PrefetchScalarGridSpec(
            num_scalar_prefetch=1,
            grid=(seqs, third // PAIR),
            in_specs=[
                part(0),
                part(third // PAIR),
                part(2 * third // PAIR),
                part(0),
                table(rows, PAIR),
                table(rows, PAIR),
                table(rows, PAIR),
                table(8, rows),
            ],
            out_specs=[part(0), table(rows, width)],
            scratch_shapes=[
                pltpu.VMEM((span, PAIR), BF16),
                pltpu.VMEM((span, PAIR), BF16),
                pltpu.VMEM((span, PAIR), BF16),
                pltpu.VMEM((span, PAIR), BF16),
                pltpu.VMEM((PAIR, span), BF16),
                pltpu.VMEM((PAIR, span), BF16),
                pltpu.VMEM((span, PAIR), jnp.int32),
                pltpu.VMEM((8, span), jnp.int32),
                pltpu.VMEM((span, PAIR), F32),
                pltpu.VMEM((span, PAIR), F32),
                pltpu.VMEM((span, PAIR), F32),
            ],
        ),
        out_shape=[
            jax.ShapeDtypeStruct((blocks, seqs, rows, third), BF16),
            jax.ShapeDtypeStruct((blocks, seqs, rows, width), BF16),
        ],
        compiler_params=pltpu.CompilerParams(vmem_limit_bytes=48 * 1024 * 1024),
        cost_estimate=pl.CostEstimate(
            flops=20_000_000_000, bytes_accessed=20_000_000, transcendentals=5_000_000
        ),
    )(order, joint, joint, joint, grad, cosine, sine, segc, segr)


def gelu_tanh(inputs):
    return jax.nn.gelu(inputs, approximate=True)


def body(
    mesh,
    tokens,
    joint_weight,
    output_weight,
    up_weight,
    down_weight,
    joint_bias,
    output_bias,
    up_bias,
    down_bias,
    norm_gain,
    norm_shift,
    segments,
    positions,
    cotangent,
):
    rows, width = tokens.shape[1], tokens.shape[2]
    hidden_width = up_weight.shape[1]
    own_rows = joint_weight.shape[0]
    devices = mesh.size
    ix, ic, izl = lax.axis_index("x"), lax.axis_index("c"), lax.axis_index("zl")
    count = 8 * rows
    heads_wide = width // 8
    units = hidden_width // 8
    own_tokens = tokens.reshape(rows, width)
    own_grad = cotangent.reshape(rows, width)

    sizes = [v.shape[0] for v in (joint_bias, up_bias, output_bias, down_bias, norm_gain, norm_shift)]
    small = lax.all_gather(
        jnp.concatenate([joint_bias, up_bias, output_bias, down_bias, norm_gain, norm_shift]), ALL
    )
    cuts = [sum(sizes[:i]) for i in range(len(sizes) + 1)]
    joint_full, up_full, output_full, down_full, gain_full, shift_full = (
        small[:, cuts[i] : cuts[i + 1]].reshape(-1).astype(F32) for i in range(6)
    )

    tokens_all = team_gather(own_tokens).reshape(count, width)
    grad_all = team_gather(own_grad).reshape(count, width)
    marks = team_gather(jnp.stack([segments.reshape(rows), positions.reshape(rows)]))

    def columns(weight):
        return weight.reshape(own_rows, 2, 2, 2, units).transpose(1, 2, 3, 0, 4)

    joint_cols = (
        joint_weight.reshape(own_rows, 3, 2, 2, 2, 2, PAIR)
        .transpose(2, 3, 5, 0, 1, 4, 6)
        .reshape(2, 2, 2, own_rows, 3 * heads_wide)
    )
    up_mine = rows_gather(exchange(columns(up_weight), TEAM), mesh).reshape(width, units)
    down_mine = rows_gather(exchange(columns(down_weight), TEAM), mesh).reshape(width, units)
    joint_mine = rows_gather(exchange(joint_cols, TEAM), mesh).reshape(width, 3 * heads_wide)
    output_mine = rows_gather(
        output_weight.reshape(1, 1, 1, own_rows, width), mesh
    ).reshape(heads_wide, width)

    joint_bias_mine = pick(
        pick(pick(joint_full.reshape(3, 2, 2, 2, 2, PAIR), ix, 1), ic, 1), izl, 2
    ).reshape(3 * heads_wide)
    up_bias_mine = pick(up_full.reshape(8, units), (ix * 2 + ic) * 2 + izl, 0)

    wide = tokens_all.astype(F32)
    centered = wide - jnp.mean(wide, 1, keepdims=True)
    inv_std = lax.rsqrt(jnp.mean(centered * centered, 1, keepdims=True) + NORM_EPS)
    normed = (centered * inv_std * gain_full + shift_full).astype(BF16)

    up_pre = dot(normed, up_mine, 1, 0) + up_bias_mine
    hidden_low = gelu_tanh(up_pre).astype(BF16)
    hidden_grad = dot(grad_all, down_mine, 1, 0)
    up_grad_low = jax.vjp(gelu_tanh, up_pre)[1](hidden_grad)[0].astype(BF16)

    joint_out = dot(normed, joint_mine, 1, 0) + joint_bias_mine
    attended_grad = dot(grad_all, output_mine, 1, 1).astype(BF16)

    marks = marks.reshape(4, 2, 2, rows)
    seg, pos = marks[:, :, 0], marks[:, :, 1]
    frequency = 10000.0 ** (-jnp.arange(0, ROT, 2, dtype=F32) / ROT)
    angles = pos.astype(F32)[..., None] * frequency
    angles = jnp.concatenate([angles, angles], -1)
    rest = angles.shape[:-1] + (HD - ROT,)
    cosine = jnp.concatenate([jnp.cos(angles), jnp.ones(rest, F32)] * 2, -1)
    sine = jnp.concatenate([jnp.sin(angles), jnp.zeros(rest, F32)] * 2, -1)
    segc = jnp.broadcast_to(seg[..., None], seg.shape + (PAIR,))
    segr = jnp.broadcast_to(seg[:, :, None], (4, 2, 8, rows))
    rel = jnp.arange(4, dtype=jnp.int32)
    order = 2 * ((rel % 2) ^ ix) + ((rel // 2) ^ ic)
    attended_low, joint_grad_low = attend(
        order.astype(jnp.int32),
        joint_out.reshape(4, 2, rows, 3 * heads_wide),
        attended_grad.reshape(4, 2, rows, heads_wide),
        cosine,
        sine,
        segc,
        segr,
    )
    attended_low = attended_low.reshape(count, heads_wide)
    joint_grad_low = joint_grad_low.reshape(count, 3 * heads_wide)

    shape = (2, 2, 2, rows, width)
    branch = dot(hidden_low, down_mine, 1, 1) + dot(attended_low, output_mine, 1, 0)
    layer_sum = team_sum(branch.astype(BF16).reshape(shape))
    layer_out = (own_tokens.astype(F32) + output_full + down_full + layer_sum).astype(BF16)
    back = dot(joint_grad_low, joint_mine, 1, 1) + dot(up_grad_low, up_mine, 1, 1)
    produced = team_sum(back.astype(BF16).reshape(shape))

    own_wide = own_tokens.astype(F32)
    own_centered = own_wide - jnp.mean(own_wide, 1, keepdims=True)
    own_inv = lax.rsqrt(jnp.mean(own_centered * own_centered, 1, keepdims=True) + NORM_EPS)
    normalized = own_centered * own_inv
    scaled = produced * gain_full
    tokens_grad = own_grad.astype(F32) + own_inv * (
        scaled
        - jnp.mean(scaled, 1, keepdims=True)
        - normalized * jnp.mean(scaled * normalized, 1, keepdims=True)
    )
    tokens_grad = tokens_grad.astype(BF16)

    rows_shape = (2, 2, 2, 2, mesh.shape["y"], own_rows)

    def to_owner(partial):
        summed = rows_sum(partial.reshape(rows_shape + (partial.shape[1],)), mesh)
        return exchange(summed.astype(BF16), TEAM).astype(F32)

    def uncolumns(value):
        return value.transpose(3, 0, 1, 2, 4).reshape(own_rows, hidden_width)

    up_weight_grad = uncolumns(to_owner(dot(normed, up_grad_low, 0, 0)))
    down_weight_grad = uncolumns(to_owner(dot(grad_all, hidden_low, 0, 0)))
    joint_weight_grad = (
        to_owner(dot(normed, joint_grad_low, 0, 0))
        .reshape(2, 2, 2, own_rows, 3, 2, PAIR)
        .transpose(3, 4, 0, 1, 5, 2, 6)
        .reshape(own_rows, 3 * width)
    )
    output_weight_grad = rows_sum(
        dot(attended_low, grad_all, 0, 0).reshape(1, 1, 2, 1, mesh.shape["y"], own_rows, width), mesh
    ).reshape(own_rows, width)

    joint_sum = jnp.sum(joint_grad_low.astype(F32), 0).reshape(3, 1, 1, 2, 1, PAIR)
    joint_sum = lax.dynamic_update_slice(
        jnp.zeros((3, 2, 2, 2, 2, PAIR), F32), joint_sum, (0, ix, ic, 0, izl, 0)
    )
    up_sum = lax.dynamic_update_slice(
        jnp.zeros((8, units), F32),
        jnp.sum(up_grad_low.astype(F32), 0)[None],
        ((ix * 2 + ic) * 2 + izl, 0),
    )
    sums = [
        joint_sum,
        up_sum,
        jnp.sum(own_grad.astype(F32), 0),
        jnp.sum(produced * normalized, 0),
        jnp.sum(produced, 0),
    ]
    sums = jnp.concatenate([v.reshape(devices, -1) for v in sums], 1)
    sums = lax.psum_scatter(sums, ALL, scatter_dimension=0)
    joint_bias_grad = sums[: cuts[1]]
    up_bias_grad = sums[cuts[1] : cuts[2]]
    grad_total, norm_gain_grad, norm_shift_grad = (
        sums[cuts[2] + i * own_rows : cuts[2] + (i + 1) * own_rows] for i in range(3)
    )
    return (
        layer_out.reshape(1, rows, width),
        tokens_grad.reshape(1, rows, width),
        joint_weight_grad,
        output_weight_grad,
        up_weight_grad,
        down_weight_grad,
        joint_bias_grad,
        grad_total,
        up_bias_grad,
        grad_total,
        norm_gain_grad,
        norm_shift_grad,
    )


def solution(mesh):
    seq, dp = mesh.shape["seq"], mesh.shape["dp"]
    fine = Mesh(mesh.devices.reshape(2, seq // 2, 2, 2, dp // 4), ALL)
    row = P(ALL, None)
    one = P(ALL)
    dp_axes, seq_axes = ("zh", "zl", "y"), ("x", "c")
    token = P(dp_axes, seq_axes, None)
    mark = P(dp_axes, seq_axes)
    return jax.shard_map(
        functools.partial(body, fine),
        mesh=fine,
        in_specs=(token,) + (row,) * 4 + (one,) * 6 + (mark, mark, token),
        out_specs=(token, token) + (row,) * 4 + (one,) * 6,
        check_vma=False,
    )
```

```python
import functools

import jax
import jax.numpy as jnp
from jax import lax
from jax.experimental import pallas as pl
from jax.experimental.pallas import tpu as pltpu
from jax.sharding import Mesh
from jax.sharding import PartitionSpec as P

ALL = ("x", "c", "zh", "zl", "y")
H = 32
HD = 64
ROT = 32
PAIR = 2 * HD
NEG_FILL = -1e30
NORM_EPS = 1e-05
F32 = jnp.float32
BF16 = jnp.bfloat16


def dot(left, right, left_dim, right_dim):
    return lax.dot_general(
        left, right, (((left_dim,), (right_dim,)), ((), ())), preferred_element_type=F32
    )


MIB = 1024 * 1024
SCALE = 0.0


def after(value, *others):
    return lax.optimization_barrier((value,) + others)[0]


def fence(*values):
    return lax.optimization_barrier(values)


def swap(value, axis):
    return lax.ppermute(value, axis, [(0, 1), (1, 0)])


def pick(value, place, dim):
    return lax.dynamic_index_in_dim(value, place, dim, keepdims=False)


def in_order(own, other, place, dim):
    return jnp.where(
        place == 0, jnp.stack([own, other], dim), jnp.stack([other, own], dim)
    )


def flip(value, place, dim):
    return jnp.where(place == 0, value, jnp.flip(value, dim))


def exchange(value):
    _, rows, n = value.shape
    return lax.all_to_all(value, ("x", "c", "zl"), 0, 0, tiled=True).reshape(4, 2, rows, n)


def fold_first(keep, other):
    value = keep.astype(F32) + other.astype(F32)
    rows, half = value.shape[0] // 4, value.shape[1] // 2
    value = value.reshape(2, 2, rows, 2 * half)
    one, two = value[..., :half], value[..., half:]
    one = one[0] + swap(one[1].astype(BF16), "x").astype(F32)
    two = two[:, 0] + swap(two[:, 1].astype(BF16), "zl").astype(F32)
    return one, two


def fold_second(halves):
    one, two = halves
    one = one[0] + swap(one[1].astype(BF16), "zl").astype(F32)
    two = two[0] + swap(two[1].astype(BF16), "x").astype(F32)
    return jnp.concatenate([one, two], 1)


def rows_first(part, mesh):
    return swap(part, "zh"), swap(part, "y") if mesh.shape["y"] == 2 else part


def rows_last(far, mesh):
    return swap(far, "y") if mesh.shape["y"] == 2 else far


def rows_pieces(part, far, side, last, mesh):
    if mesh.shape["y"] == 2:
        return part, far, side, last
    value = in_order(part, far, lax.axis_index("zh"), 1)
    return (lax.all_gather(value, "y", axis=3).reshape(-1, part.shape[-1]),)


def zh_halves(value):
    place = lax.axis_index("zh")
    return pick(value, place, 2).astype(F32), pick(value, 1 - place, 2).astype(BF16)


def to_owner(summed):
    value = summed.astype(BF16).reshape((8,) + summed.shape[3:])
    return lax.all_to_all(value, ("x", "c", "zl"), 0, 0, tiled=True)


def rows_sum(value, mesh):
    if mesh.shape["y"] != 2:
        value = lax.psum_scatter(value.astype(BF16), "y", scatter_dimension=4)
    else:
        place = lax.axis_index("y")
        other = swap(pick(value, 1 - place, 4).astype(BF16), "y")
        value = pick(value, place, 4).astype(F32) + other.astype(F32)
    keep, send = zh_halves(value)
    return keep + swap(send, "zh").astype(F32)


def spread(value, devices):
    return lax.all_to_all(
        jnp.broadcast_to(value[None], (devices,) + value.shape), ALL, 0, 0, tiled=True
    )


def params(**kind):
    return pltpu.CompilerParams(vmem_limit_bytes=56 * MIB, **kind)


def cost(units):
    return pl.CostEstimate(flops=int(units * SCALE * 1e9), bytes_accessed=0, transcendentals=0)


HBM = pl.BlockSpec(memory_space=pl.ANY)
SCALARS = pl.BlockSpec(memory_space=pltpu.SMEM)


def load_rows(place, pieces, out, sems):
    if len(pieces) == 1:
        copies = [pltpu.make_async_copy(pieces[0], out, sems.at[0])]
    else:
        xc, zl, rows, _ = pieces[0].shape
        copies = []
        for i, piece in enumerate(pieces):
            zh, y = place[0] ^ (i % 2), place[1] ^ (i // 2)
            for j in range(xc):
                for k in range(zl):
                    row = (((j * 2 + zh) * zl + k) * 2 + y) * rows
                    row = pl.ds(pl.multiple_of(row, rows), rows)
                    copies.append(
                        pltpu.make_async_copy(
                            piece.at[j, k], out.at[row, :], sems.at[len(copies)]
                        )
                    )
    for copy in copies:
        copy.start()
    return copies


def weight_specs(*weights):
    return [HBM for weight in weights for _ in weight]


def weight_scratch(*weights):
    shapes = []
    for weight in weights:
        n = weight[0].shape[-1]
        rows = sum(piece.size for piece in weight) // n
        shapes += [pltpu.VMEM((rows, n), BF16), pltpu.SemaphoreType.DMA((32,))]
    return shapes


def own_place():
    return jnp.stack([lax.axis_index("zh"), lax.axis_index("y")]).astype(jnp.int32)


def at_first(refs, place, counts, scratch):
    @pl.when(pl.program_id(0) == 0)
    def _():
        copies, first = [], 0
        for i, count in enumerate(counts):
            copies += load_rows(place, refs[first : first + count], *scratch[2 * i : 2 * i + 2])
            first += count
        for copy in copies:
            copy.wait()


GELU_A = 0.7978845608028654
GELU_B = 0.044715
CHUNK = 256


def up_kernel(place, normed, bias, *refs):
    count = len(refs) - 4
    pieces, (pre, hidden, weight, sems) = refs[:count], refs[count:]
    at_first(pieces, place, (count,), (weight, sems))
    for first in range(0, weight.shape[1], CHUNK):
        part = slice(first, first + CHUNK)
        value = dot(normed[...], weight[:, part], 1, 0) + bias[:, part]
        pre[:, part] = value
        inner = jnp.tanh(GELU_A * (value + GELU_B * (value * value * value)))
        hidden[:, part] = (0.5 * value * (1.0 + inner)).astype(BF16)


def up_forward(normed, bias, weight, block):
    count, width = normed.shape
    n = weight[0].shape[-1]
    return pl.pallas_call(
        up_kernel,
        grid=(count // block,),
        in_specs=[
            SCALARS,
            pl.BlockSpec((block, width), lambda i: (i, 0)),
            pl.BlockSpec((1, n), lambda i: (0, 0)),
        ]
        + weight_specs(weight),
        out_specs=[pl.BlockSpec((block, n), lambda i: (i, 0))] * 2,
        out_shape=[jax.ShapeDtypeStruct((count, n), F32), jax.ShapeDtypeStruct((count, n), BF16)],
        scratch_shapes=weight_scratch(weight),
        compiler_params=params(),
        cost_estimate=cost(17),
    )(own_place(), normed, bias, *weight)


def hidden_grad_kernel(place, grad, pre, *refs):
    count = len(refs) - 4
    pieces, (out, total, weight, sems) = refs[:count], refs[count:]
    at_first(pieces, place, (count,), (weight, sems))

    @pl.when(pl.program_id(0) == 0)
    def _():
        total[...] = jnp.zeros_like(total)

    for first in range(0, weight.shape[1], CHUNK):
        part = slice(first, first + CHUNK)
        value = pre[:, part]
        square = value * value
        inner = jnp.tanh(GELU_A * (value + GELU_B * (square * value)))
        slope = 0.5 * (1.0 + inner) + 0.5 * value * (1.0 - inner * inner) * (
            GELU_A * (1.0 + 3.0 * GELU_B * square)
        )
        low = (dot(grad[...], weight[:, part], 1, 0) * slope).astype(BF16)
        out[:, part] = low
        total[:, part] += jnp.sum(low.astype(F32), 0, keepdims=True)


def hidden_backward(grad, pre, weight, block):
    count, width = grad.shape
    n = weight[0].shape[-1]
    return pl.pallas_call(
        hidden_grad_kernel,
        grid=(count // block,),
        in_specs=[
            SCALARS,
            pl.BlockSpec((block, width), lambda i: (i, 0)),
            pl.BlockSpec((block, n), lambda i: (i, 0)),
        ]
        + weight_specs(weight),
        out_specs=[
            pl.BlockSpec((block, n), lambda i: (i, 0)),
            pl.BlockSpec((1, n), lambda i: (0, 0)),
        ],
        out_shape=[jax.ShapeDtypeStruct((count, n), BF16), jax.ShapeDtypeStruct((1, n), F32)],
        scratch_shapes=weight_scratch(weight),
        compiler_params=params(),
        cost_estimate=cost(20),
    )(own_place(), grad, pre, *weight)


def weight_grad_kernel(place, left, right, keep, send):
    xc, zh, zl, rows, n = keep.shape
    value = dot(left[...], right[...], 0, 0).astype(BF16).reshape(zl, 2, rows, n)
    own = place[1] == 0
    keep[0, 0] = jnp.where(own, value[:, 0], value[:, 1])
    send[0, 0] = jnp.where(own, value[:, 1], value[:, 0])


def weight_grad_plain_kernel(left, right, out):
    out[...] = dot(left[...], right[...], 0, 0).astype(BF16)


def weight_grad(left, right, mesh):
    count, width = left.shape
    n = right.shape[1]
    y = mesh.shape["y"]
    rows = width // (16 * y)
    block = width // 8
    specs = [
        pl.BlockSpec((count, block), lambda i: (0, i)),
        pl.BlockSpec((count, n), lambda i: (0, 0), pipeline_mode=pl.Buffered(1)),
    ]
    if y != 2:
        full = pl.pallas_call(
            weight_grad_plain_kernel,
            grid=(8,),
            in_specs=specs,
            out_specs=pl.BlockSpec((block, n), lambda i: (i, 0)),
            out_shape=jax.ShapeDtypeStruct((width, n), BF16),
            compiler_params=params(),
            cost_estimate=cost(14 * n / 1024),
        )(left, right)
        return full, full
    out = pl.BlockSpec((1, 1, 2, rows, n), lambda i: (i // 2, i % 2, 0, 0, 0))
    shape = jax.ShapeDtypeStruct((4, 2, 2, rows, n), BF16)
    keep, send = pl.pallas_call(
        weight_grad_kernel,
        grid=(8,),
        in_specs=[SCALARS] + specs,
        out_specs=[out, out],
        out_shape=[shape, shape],
        compiler_params=params(),
        cost_estimate=cost(14 * n / 1024),
    )(own_place(), left, right)

    return keep, send


def sum_first(send, mesh):
    if mesh.shape["y"] == 2:
        return swap(send, "y")
    y, n = mesh.shape["y"], send.shape[-1]
    rows = send.shape[0] // (16 * y)
    return lax.psum_scatter(send.reshape(2, 2, 2, 2, y, rows, n), "y", scatter_dimension=4)


def sum_halves(keep, other, mesh):
    if mesh.shape["y"] != 2:
        return zh_halves(other)
    value = keep.astype(F32) + other.astype(F32)
    return zh_halves(value.reshape((2, 2, 2, 2) + value.shape[3:]))


def joint_kernel(place, normed, bias, cosine, sine, *refs):
    count = len(refs) - 3
    pieces, (out, weight, sems) = refs[:count], refs[count:]
    at_first(pieces, place, (count,), (weight, sems))
    value = dot(normed[...], weight[...], 1, 0) + bias[...]
    third = value.shape[1] // 3
    lane = lax.broadcasted_iota(jnp.int32, (value.shape[0], PAIR), 1) % HD
    for first in range(0, 2 * third, PAIR):
        piece = turn(value[:, first : first + PAIR], cosine[...], sine[...], lane, 1.0).astype(BF16)
        if first < third:
            piece = piece * jnp.asarray(HD ** (-0.5), BF16)
        out[:, first : first + PAIR] = piece
    out[:, 2 * third :] = value[:, 2 * third :].astype(BF16)


def joint_forward(normed, bias, cosine, sine, weight, block):
    count, width = normed.shape
    n = weight[0].shape[-1]
    return pl.pallas_call(
        joint_kernel,
        grid=(count // block,),
        in_specs=[
            SCALARS,
            pl.BlockSpec((block, width), lambda i: (i, 0)),
            pl.BlockSpec((1, n), lambda i: (0, 0)),
            pl.BlockSpec((block, PAIR), lambda i: (i, 0)),
            pl.BlockSpec((block, PAIR), lambda i: (i, 0)),
        ]
        + weight_specs(weight),
        out_specs=pl.BlockSpec((block, n), lambda i: (i, 0)),
        out_shape=jax.ShapeDtypeStruct((count, n), BF16),
        scratch_shapes=weight_scratch(weight),
        compiler_params=params(),
        cost_estimate=cost(13.5),
    )(own_place(), normed, bias, cosine, sine, *weight)


def pair_kernel(dims, counts, place, one, two, *refs):
    total = sum(counts)
    pieces, (keep, send), scratch = refs[:total], refs[total : total + 2], refs[total + 2 :]
    at_first(pieces, place, counts, scratch)

    def step(out):
        for first in range(0, out.shape[1], 2 * CHUNK):
            part = slice(first, first + 2 * CHUNK)
            value = 0.0
            for left, right, dim in zip((one, two), (scratch[0], scratch[2]), dims):
                right = right[part, :] if dim == 1 else right[:, part]
                value = value + dot(left[...], right, 1, dim)
            out[:, part] = value.astype(BF16)

    half = pl.num_programs(0) // 2
    pl.when(pl.program_id(0) < half)(lambda: step(keep))
    pl.when(pl.program_id(0) >= half)(lambda: step(send))


def pair_product(one, first, two, second, dims, block, units):
    count = one.shape[0]
    width = first[0].shape[-1] if dims[0] == 0 else sum(p.size for p in first) // first[0].shape[-1]
    steps = count // block
    shape = jax.ShapeDtypeStruct((count // 2, width), BF16)
    return pl.pallas_call(
        functools.partial(pair_kernel, dims, (len(first), len(second))),
        grid=(steps,),
        in_specs=[
            SCALARS,
            pl.BlockSpec((block, one.shape[1]), lambda i: (i, 0)),
            pl.BlockSpec((block, two.shape[1]), lambda i: (i, 0)),
        ]
        + weight_specs(first, second),
        out_specs=[
            pl.BlockSpec((block, width), lambda i: (jnp.minimum(i, steps // 2 - 1), 0)),
            pl.BlockSpec((block, width), lambda i: (jnp.maximum(i - steps // 2, 0), 0)),
        ],
        out_shape=[shape, shape],
        scratch_shapes=weight_scratch(first, second),
        compiler_params=params(),
        cost_estimate=cost(units),
    )(own_place(), one, two, *first, *second)


def norm_kernel(*refs):
    blocks, (gain_ref, shift_ref, out_ref) = refs[:8], refs[8:]

    def one(ref):
        wide = ref[...].astype(F32)
        centered = wide - jnp.mean(wide, 1, keepdims=True)
        inv_std = lax.rsqrt(jnp.mean(centered * centered, 1, keepdims=True) + NORM_EPS)
        out_ref[...] = (centered * inv_std * gain_ref[...] + shift_ref[...]).astype(BF16)

    for i, ref in enumerate(blocks):
        pl.when(pl.program_id(0) == i)(functools.partial(one, ref))


def grad_kernel(*refs):
    blocks, (weight_ref, out_ref, attended_ref) = refs[:8], refs[8:]

    def one(ref):
        out_ref[...] = ref[...]
        attended_ref[...] = dot(ref[...], weight_ref[...], 1, 1).astype(BF16)

    for i, ref in enumerate(blocks):
        pl.when(pl.program_id(0) == i)(functools.partial(one, ref))


def rows_of_team(kernel, blocks, rest, widths):
    rows = blocks[0].shape[0]
    return pl.pallas_call(
        kernel,
        grid=(8,),
        in_specs=[
            pl.BlockSpec(value.shape, lambda i: (0, 0), pipeline_mode=pl.Buffered(1))
            for value in (*blocks, *rest)
        ],
        out_specs=[pl.BlockSpec((rows, wide), lambda i: (i, 0)) for wide in widths],
        out_shape=[jax.ShapeDtypeStruct((8 * rows, wide), BF16) for wide in widths],
        compiler_params=params(),
        cost_estimate=cost(11),
    )(*blocks, *rest)


def split_kernel(value, out):
    n = out.shape[2]
    for i in range(8):
        out[i] = value[:, i * n : (i + 1) * n]


def join_kernel(value, out):
    n = value.shape[2]
    for i in range(8):
        out[:, i * n : (i + 1) * n] = value[i].astype(F32)


def by_columns(weight):
    rows, n = weight.shape[0], weight.shape[1] // 8
    return pl.pallas_call(
        split_kernel,
        out_shape=jax.ShapeDtypeStruct((8, rows, n), weight.dtype),
        cost_estimate=cost(2),
    )(weight)


def from_columns(value):
    _, rows, n = value.shape
    return pl.pallas_call(
        join_kernel,
        out_shape=jax.ShapeDtypeStruct((rows, 8 * n), F32),
        cost_estimate=cost(3),
    )(value)


def head_places():
    for third in range(3):
        for x in range(2):
            for c in range(2):
                for zh in range(2):
                    for zl in range(2):
                        pair = ((x * 2 + c) * 2 + zh) * 2 + zl
                        yield (x * 2 + c) * 2 + zl, (third * 2 + zh) * PAIR, (third * 16 + pair) * PAIR


def split_heads_kernel(value, out):
    for place, own, whole in head_places():
        out[place, :, own : own + PAIR] = value[:, whole : whole + PAIR]


def join_heads_kernel(value, out):
    for place, own, whole in head_places():
        out[:, whole : whole + PAIR] = value[place, :, own : own + PAIR].astype(F32)


def by_heads(weight):
    rows, n = weight.shape[0], weight.shape[1] // 8
    return pl.pallas_call(
        split_heads_kernel,
        out_shape=jax.ShapeDtypeStruct((8, rows, n), weight.dtype),
        cost_estimate=cost(2),
    )(weight)


def from_heads(value):
    _, rows, n = value.shape
    return pl.pallas_call(
        join_heads_kernel,
        out_shape=jax.ShapeDtypeStruct((rows, 8 * n), F32),
        cost_estimate=cost(3),
    )(value)


def rows_sorted(pieces, mesh):
    if len(pieces) == 1:
        return pieces[0]
    zh, y = lax.axis_index("zh"), lax.axis_index("y")
    n = pieces[0].shape[-1]
    near = in_order(pieces[0], pieces[1], zh, 1)
    side = in_order(pieces[2], pieces[3], zh, 1)
    return in_order(near, side, y, 3).reshape(-1, n)


def turn(value, cosine, sine, lane, sign):
    half = ROT // 2
    width = value.shape[-1]
    up = pltpu.roll(value, width - half, 1)
    down = pltpu.roll(value, half, 1)
    turned = jnp.where(lane < half, -up, down)
    return value * cosine + (sign * turned) * sine


def attend_kernel(
    order, q_ref, k_ref, v_ref, do_ref, cos_ref, sin_ref, segc_ref, segr_ref,
    out_ref, grad_ref, qs, ks, vs, ds, kt, vt, segc, segr, dq, dk, dv,
):
    rows = q_ref.shape[2]
    blocks = q_ref.shape[0]
    pair = pl.program_id(1)
    scale = HD ** (-0.5)
    lane = lax.broadcasted_iota(jnp.int32, (rows, PAIR), 1) % HD

    def place(block):
        return pl.ds(pl.multiple_of(order[block] * rows, rows), rows)

    for block in range(blocks):
        at = place(block)
        qs[at, :] = q_ref[block, 0]
        ks[at, :] = k_ref[block, 0]
        kt[:, at] = k_ref[block, 0].T
        vs[at, :] = v_ref[block, 0]
        vt[:, at] = v_ref[block, 0].T
        ds[at, :] = do_ref[block, 0]
        segc[at, :] = segc_ref[block, 0]
        segr[:, at] = segr_ref[block, 0]
    dk[...] = jnp.zeros_like(dk)
    dv[...] = jnp.zeros_like(dv)
    side = lax.broadcasted_iota(jnp.int32, (rows, PAIR), 1) // HD
    causal = lax.broadcasted_iota(jnp.int32, (rows, rows), 0) <= lax.broadcasted_iota(
        jnp.int32, (rows, rows), 1
    )
    for block in range(blocks):
        here = slice(block * rows, (block + 1) * rows)
        count = (block + 1) * rows
        same = segc[:count, :1] == segr[:1, here]
        if block == 0:
            allowed = same & causal
        else:
            allowed = jnp.concatenate([same[: count - rows], same[count - rows :] & causal], 0)
        query, grad = qs[here, :], ds[here, :]
        tops = []
        turns = []
        for head in range(2):
            lanes = slice(head * HD, (head + 1) * HD)
            query_one = jnp.where(side == head, query, jnp.zeros_like(query))
            grad_one = jnp.where(side == head, grad, jnp.zeros_like(grad))
            scores = dot(ks[:count, :], query_one, 1, 1)
            scores = jnp.where(allowed, scores, NEG_FILL)
            exps = jnp.exp(scores - jnp.max(scores, 0, keepdims=True))
            probs = exps * (1.0 / jnp.sum(exps, 0, keepdims=True))
            probs_low = probs.astype(BF16)
            tops.append(dot(vt[lanes, :count], probs_low, 1, 0))
            dv[:count, :] += dot(probs_low, grad_one, 1, 0)
            probs_grad = dot(vs[:count, :], grad_one, 1, 1)
            inner = jnp.sum(probs * probs_grad, 0, keepdims=True)
            score_grad = (probs * (probs_grad - inner)).astype(BF16)
            dk[:count, :] += dot(score_grad, query_one, 1, 0)
            turns.append(dot(kt[lanes, :count], score_grad, 1, 0))
        ds[here, :] = jnp.concatenate(tops, 0).T.astype(BF16)
        dq[here, :] = (jnp.concatenate(turns, 0) * scale).T
    for block in range(blocks):
        at = place(block)
        cosine, sine = cos_ref[block, 0], sin_ref[block, 0]
        out_ref[block, 0] = ds[at, :]
        for part, source in enumerate((dq, dk)):
            spot = pl.ds(pl.multiple_of(part * 2 * PAIR + pair * PAIR, PAIR), PAIR)
            grad_ref[block, 0, :, spot] = turn(source[at, :], cosine, sine, lane, -1.0).astype(BF16)
        spot = pl.ds(pl.multiple_of(4 * PAIR + pair * PAIR, PAIR), PAIR)
        grad_ref[block, 0, :, spot] = dv[at, :].astype(BF16)


def attend(order, joint, grad, cosine, sine, segc, segr):
    blocks, seqs, rows, width = joint.shape
    span = blocks * rows
    third = width // 3

    def part(first):
        return pl.BlockSpec((blocks, 1, rows, PAIR), lambda s, p, o: (0, s, 0, first + p))

    def table(height, wide):
        return pl.BlockSpec((blocks, 1, height, wide), lambda s, p, o: (0, s, 0, 0))

    return pl.pallas_call(
        attend_kernel,
        grid_spec=pltpu.PrefetchScalarGridSpec(
            num_scalar_prefetch=1,
            grid=(seqs, third // PAIR),
            in_specs=[
                part(0),
                part(third // PAIR),
                part(2 * third // PAIR),
                part(0),
                table(rows, PAIR),
                table(rows, PAIR),
                table(rows, PAIR),
                table(8, rows),
            ],
            out_specs=[part(0), table(rows, width)],
            scratch_shapes=[
                pltpu.VMEM((span, PAIR), BF16),
                pltpu.VMEM((span, PAIR), BF16),
                pltpu.VMEM((span, PAIR), BF16),
                pltpu.VMEM((span, PAIR), BF16),
                pltpu.VMEM((PAIR, span), BF16),
                pltpu.VMEM((PAIR, span), BF16),
                pltpu.VMEM((span, PAIR), jnp.int32),
                pltpu.VMEM((8, span), jnp.int32),
                pltpu.VMEM((span, PAIR), F32),
                pltpu.VMEM((span, PAIR), F32),
                pltpu.VMEM((span, PAIR), F32),
            ],
        ),
        out_shape=[
            jax.ShapeDtypeStruct((blocks, seqs, rows, third), BF16),
            jax.ShapeDtypeStruct((blocks, seqs, rows, width), BF16),
        ],
        compiler_params=params(),
        cost_estimate=cost(33),
    )(order, joint, joint, joint, grad, cosine, sine, segc, segr)


def body(
    mesh,
    tokens,
    joint_weight,
    output_weight,
    up_weight,
    down_weight,
    joint_bias,
    output_bias,
    up_bias,
    down_bias,
    norm_gain,
    norm_shift,
    segments,
    positions,
    cotangent,
):
    rows, width = tokens.shape[1], tokens.shape[2]
    hidden_width = up_weight.shape[1]
    own_rows = joint_weight.shape[0]
    devices = mesh.size
    ix, ic, izl = (lax.axis_index(axis) for axis in ("x", "c", "zl"))
    count = 8 * rows
    heads_wide = width // 8
    units = hidden_width // 8
    own_tokens = tokens.reshape(rows, width)
    own_grad = cotangent.reshape(rows, width)

    sizes = [v.shape[0] for v in (joint_bias, up_bias, output_bias, down_bias, norm_gain, norm_shift)]
    cuts = [sum(sizes[:i]) for i in range(len(sizes) + 1)]
    small = jnp.concatenate(
        [
            value.astype(F32)
            for value in (joint_bias, up_bias, output_bias, down_bias, norm_gain, norm_shift)
        ]
        + [segments.reshape(rows).astype(F32), positions.reshape(rows).astype(F32)]
    )
    lines = -(-small.shape[0] // 128)
    small = jnp.pad(small, (0, lines * 128 - small.shape[0])).reshape(lines, 128)
    block = 2 * rows
    output_part = output_weight.reshape(1, 1, own_rows, width)
    up_part = exchange(by_columns(up_weight))
    output_far, output_side = rows_first(output_part, mesh)
    others = jnp.concatenate([by_columns(down_weight), by_heads(joint_weight)], 2)
    small = spread(small, devices)
    up_part, output_far, output_side, others, token, small = fence(
        up_part, output_far, output_side, others, own_tokens, small
    )

    up_far, up_side = rows_first(up_part, mesh)
    token_near, token_far = swap(token, "zl"), swap(token, "x")
    output_last = rows_last(output_far, mesh)
    others = exchange(others)
    up_far, up_side, token_near, token_far, output_last, grad, others = fence(
        up_far, up_side, token_near, token_far, output_last, own_grad, others
    )
    down_part, joint_part = others[..., :units], others[..., units:]

    down_far, down_side = rows_first(down_part, mesh)
    up_last = rows_last(up_far, mesh)
    both = swap(jnp.stack([token_near, grad]), "x")
    grad_near = swap(grad, "zl")
    small = small.reshape(devices, lines * 128)
    joint_full, up_full, output_full, down_full, gain_full, shift_full = (
        small[:, cuts[i] : cuts[i + 1]].reshape(-1) for i in range(6)
    )
    marks = small[:, cuts[6] : cuts[6] + 2 * rows].reshape(2, 2, 2, 2, mesh.shape["y"], 2, rows)
    marks = pick(pick(marks, lax.axis_index("zh"), 2), lax.axis_index("y"), 3)
    marks = flip(flip(flip(marks, ix, 0), ic, 1), izl, 2)
    marks = marks.transpose(1, 0, 2, 3, 4).reshape(4, 2, 2, rows)
    joint_bias_mine = pick(
        pick(pick(joint_full.reshape(3, 2, 2, 2, 2, PAIR), ix, 1), ic, 1), izl, 2
    ).reshape(1, 3 * heads_wide)
    up_bias_mine = pick(up_full.reshape(8, 1, units), (ix * 2 + ic) * 2 + izl, 0)
    gain_row, shift_row = gain_full.reshape(1, width), shift_full.reshape(1, width)
    seg, pos = marks[:, :, 0].astype(jnp.int32), marks[:, :, 1]
    frequency = 10000.0 ** (-jnp.arange(0, ROT, 2, dtype=F32) / ROT)
    angles = pos[..., None] * frequency
    angles = jnp.concatenate([angles, angles], -1)
    rest = angles.shape[:-1] + (HD - ROT,)
    cosine = jnp.concatenate([jnp.cos(angles), jnp.ones(rest, F32)] * 2, -1)
    sine = jnp.concatenate([jnp.sin(angles), jnp.zeros(rest, F32)] * 2, -1)
    segc = jnp.broadcast_to(seg[..., None], seg.shape + (PAIR,))
    segr = jnp.broadcast_to(seg[:, :, None], (4, 2, 8, rows))
    rel = jnp.arange(4, dtype=jnp.int32)
    order = (2 * ((rel % 2) ^ ix) + ((rel // 2) ^ ic)).astype(jnp.int32)
    output_mine = rows_sorted(
        rows_pieces(output_part, output_far, output_side, output_last, mesh), mesh
    )
    (
        down_far, down_side, up_last, both, joint_part, grad_near,
        cosine, sine, segc, segr, output_mine, gain_row, shift_row, up_bias_mine,
    ) = fence(
        down_far, down_side, up_last, both, joint_part, grad_near,
        cosine, sine, segc, segr, output_mine, gain_row, shift_row, up_bias_mine,
    )
    tokens = (token, token_near, token_far, both[0])
    tokens += tuple(swap(v, "c") for v in tokens)
    tokens, down_far, joint_part, grad, grad_near, grad_far = fence(
        tokens, down_far, joint_part, grad, grad_near, both[1]
    )

    joint_far, joint_side = rows_first(joint_part, mesh)
    down_last = rows_last(down_far, mesh)
    grad_last = swap(grad_near, "x")
    (normed,) = rows_of_team(norm_kernel, tokens, (gain_row, shift_row), (width,))
    up_mine = rows_pieces(up_part, up_far, up_side, up_last, mesh)
    up_pre, hidden_low = up_forward(normed, up_bias_mine, up_mine, block)
    joint_far, joint_side, down_last, grad_last, hidden_low, normed = fence(
        joint_far, joint_side, down_last, grad_last, hidden_low, normed
    )
    grads = (grad, grad_near, grad_far, grad_last)
    grads += tuple(swap(v, "c") for v in grads)
    grads, joint_far = fence(grads, joint_far)

    joint_last = rows_last(joint_far, mesh)
    grad_all, attended_grad = rows_of_team(
        grad_kernel,
        grads,
        (output_mine,),
        (width, heads_wide),
    )
    down_mine = rows_pieces(down_part, down_far, down_side, down_last, mesh)
    down_keep, down_send = weight_grad(grad_all, hidden_low, mesh)
    down_send, grad_all, attended_grad, joint_last = fence(
        down_send, grad_all, attended_grad, joint_last
    )

    down_other = sum_first(down_send, mesh)
    up_grad_low, up_total = hidden_backward(grad_all, up_pre, down_mine, block)
    up_keep, up_send = weight_grad(normed, up_grad_low, mesh)
    joint_mine = rows_pieces(joint_part, joint_far, joint_side, joint_last, mesh)
    joint_low = joint_forward(
        after(normed, up_send),
        joint_bias_mine,
        cosine.reshape(count, PAIR),
        sine.reshape(count, PAIR),
        joint_mine,
        block,
    )
    down_other, up_send, joint_low, up_grad_low = fence(down_other, up_send, joint_low, up_grad_low)

    up_other = sum_first(up_send, mesh)
    down_keep, down_send = sum_halves(down_keep, down_other, mesh)
    down_other = swap(down_send, "zh")
    attended_low, joint_grad_low = attend(
        order,
        joint_low.reshape(4, 2, rows, 3 * heads_wide),
        attended_grad.reshape(4, 2, rows, heads_wide),
        cosine,
        sine,
        segc,
        segr,
    )
    attended_low = attended_low.reshape(count, heads_wide)
    joint_grad_low = joint_grad_low.reshape(count, 3 * heads_wide)
    joint_keep, joint_send = weight_grad(normed, joint_grad_low, mesh)
    up_other, down_other, down_keep, attended_low, joint_grad_low, joint_send = fence(
        up_other, down_other, down_keep, attended_low, joint_grad_low, joint_send
    )

    joint_other = sum_first(joint_send, mesh)
    up_keep, up_send = sum_halves(up_keep, up_other, mesh)
    up_other = swap(up_send, "zh")
    down_moved = to_owner(down_keep + down_other.astype(F32))
    back_keep, back_send = pair_product(
        joint_grad_low, joint_mine, up_grad_low, up_mine, (1, 1), block, 24
    )
    out_keep, out_send = pair_product(
        after(hidden_low, back_send), down_mine, attended_low, (output_mine,), (1, 0), block, 19
    )
    back_other = swap(back_send, "c")
    joint_other, up_other, up_keep, down_moved, back_keep, back_other, out_send = fence(
        joint_other, up_other, up_keep, down_moved, back_keep, back_other, out_send
    )

    joint_keep, joint_send = sum_halves(joint_keep, joint_other, mesh)
    joint_other = swap(joint_send, "zh")
    up_moved = to_owner(up_keep + up_other.astype(F32))
    out_other = swap(out_send, "c")
    back = fold_first(back_keep, back_other)
    output_grad = dot(attended_low, grad_all, 0, 0).astype(BF16)
    joint_other, joint_keep, up_moved, out_other, back, output_grad = fence(
        joint_other, joint_keep, up_moved, out_other, back, output_grad
    )

    joint_moved = to_owner(joint_keep + joint_other.astype(F32))
    produced = fold_second(back)
    out = fold_first(out_keep, out_other)
    output_weight_grad = rows_sum(
        output_grad.reshape(1, 1, 2, 1, mesh.shape["y"], own_rows, width), mesh
    ).reshape(own_rows, width)
    joint_moved, out, produced = fence(joint_moved, out, produced)
    layer_sum = fold_second(out)
    layer_out = (own_tokens.astype(F32) + output_full + down_full + layer_sum).astype(BF16)
    own_wide = own_tokens.astype(F32)
    own_centered = own_wide - jnp.mean(own_wide, 1, keepdims=True)
    own_inv = lax.rsqrt(jnp.mean(own_centered * own_centered, 1, keepdims=True) + NORM_EPS)
    normalized = own_centered * own_inv
    scaled = produced * gain_full
    tokens_grad = own_grad.astype(F32) + own_inv * (
        scaled
        - jnp.mean(scaled, 1, keepdims=True)
        - normalized * jnp.mean(scaled * normalized, 1, keepdims=True)
    )
    tokens_grad = tokens_grad.astype(BF16)

    down_weight_grad = from_columns(down_moved)
    joint_weight_grad = from_heads(joint_moved)
    up_weight_grad = from_columns(up_moved)
    joint_sum = jnp.sum(joint_grad_low.astype(F32), 0).reshape(3, 1, 1, 2, 1, PAIR)
    joint_sum = lax.dynamic_update_slice(
        jnp.zeros((3, 2, 2, 2, 2, PAIR), F32), joint_sum, (0, ix, ic, 0, izl, 0)
    )
    up_sum = lax.dynamic_update_slice(
        jnp.zeros((8, units), F32), up_total, ((ix * 2 + ic) * 2 + izl, 0)
    )
    sums = [
        joint_sum,
        up_sum,
        jnp.sum(own_grad.astype(F32), 0),
        jnp.sum(produced * normalized, 0),
        jnp.sum(produced, 0),
    ]
    sums = jnp.concatenate([v.reshape(devices, -1) for v in sums], 1)
    sums = lax.all_to_all(sums, ALL, 0, 0, tiled=True)
    sums = jnp.sum(sums, 0)
    joint_bias_grad = sums[: cuts[1]]
    up_bias_grad = sums[cuts[1] : cuts[2]]
    grad_total, norm_gain_grad, norm_shift_grad = (
        sums[cuts[2] + i * own_rows : cuts[2] + (i + 1) * own_rows] for i in range(3)
    )
    return (
        layer_out.reshape(1, rows, width),
        tokens_grad.reshape(1, rows, width),
        joint_weight_grad,
        output_weight_grad,
        up_weight_grad,
        down_weight_grad,
        joint_bias_grad,
        grad_total,
        up_bias_grad,
        grad_total,
        norm_gain_grad,
        norm_shift_grad,
    )


def solution(mesh):
    seq, dp = mesh.shape["seq"], mesh.shape["dp"]
    fine = Mesh(mesh.devices.reshape(2, seq // 2, 2, 2, dp // 4), ALL)
    row = P(ALL, None)
    one = P(ALL)
    dp_axes, seq_axes = ("zh", "zl", "y"), ("x", "c")
    token = P(dp_axes, seq_axes, None)
    mark = P(dp_axes, seq_axes)
    return jax.shard_map(
        functools.partial(body, fine),
        mesh=fine,
        in_specs=(token,) + (row,) * 4 + (one,) * 6 + (mark, mark, token),
        out_specs=(token, token) + (row,) * 4 + (one,) * 6,
        check_vma=False,
    )
```

```python
import functools

import jax
import jax.numpy as jnp
from jax import lax
from jax.experimental import pallas as pl
from jax.experimental.pallas import tpu as pltpu
from jax.sharding import Mesh
from jax.sharding import PartitionSpec as P

ALL = ("x", "c", "zh", "zl", "y")
H = 32
HD = 64
ROT = 32
PAIR = 2 * HD
NEG_FILL = -1e30
NORM_EPS = 1e-05
F32 = jnp.float32
BF16 = jnp.bfloat16


def dot(left, right, left_dim, right_dim):
    return lax.dot_general(
        left, right, (((left_dim,), (right_dim,)), ((), ())), preferred_element_type=F32
    )


MIB = 1024 * 1024
SCALE = 0.0


def after(value, *others):
    return lax.optimization_barrier((value,) + others)[0]


def fence(*values):
    return lax.optimization_barrier(values)


def swap(value, axis):
    return lax.ppermute(value, axis, [(0, 1), (1, 0)])


def pick(value, place, dim):
    return lax.dynamic_index_in_dim(value, place, dim, keepdims=False)


def in_order(own, other, place, dim):
    return jnp.where(
        place == 0, jnp.stack([own, other], dim), jnp.stack([other, own], dim)
    )


def flip(value, place, dim):
    return jnp.where(place == 0, value, jnp.flip(value, dim))


def exchange(value):
    _, rows, n = value.shape
    return lax.all_to_all(value, ("x", "c", "zl"), 0, 0, tiled=True).reshape(4, 2, rows, n)


def fold_first(keep, other):
    rows, half = keep.shape[0] // 4, keep.shape[1] // 2
    keep, other = (value.reshape(2, 2, rows, 2 * half) for value in (keep, other))

    def part(x, zl, columns):
        return keep[x, zl, :, columns].astype(F32) + other[x, zl, :, columns].astype(F32)

    one, two = slice(0, half), slice(half, 2 * half)
    send_one = jnp.stack([part(1, 0, one), part(1, 1, one)]).astype(BF16)
    send_two = jnp.stack([part(0, 1, two), part(1, 1, two)]).astype(BF16)
    other_one, other_two = swap(send_one, "x"), swap(send_two, "zl")
    return (
        part(0, 0, one) + other_one[0].astype(F32),
        (part(0, 1, one) + other_one[1].astype(F32)).astype(BF16),
        part(0, 0, two) + other_two[0].astype(F32),
        (part(1, 0, two) + other_two[1].astype(F32)).astype(BF16),
    )


def fold_second(parts):
    one, send_one, two, send_two = parts
    one = one + swap(send_one, "zl").astype(F32)
    two = two + swap(send_two, "x").astype(F32)
    return jnp.concatenate([one, two], 1)


def pause_kernel(value, out):
    out[...] = value[...]


def far_swap(value):
    other = swap(value, "zh")
    lead = (1,) * (value.ndim - 2)
    paused = pl.pallas_call(
        pause_kernel,
        grid=(1,),
        in_specs=[pl.BlockSpec(lead + (16, 128), lambda i: (0,) * value.ndim)],
        out_specs=pl.BlockSpec(lead + (16, 128), lambda i: (0,) * value.ndim),
        out_shape=jax.ShapeDtypeStruct(lead + (16, 128), BF16),
        cost_estimate=pl.CostEstimate(
            flops=60_000_000_000, bytes_accessed=0, transcendentals=0
        ),
    )(other)
    return after(other, paused)


def rows_first(part, mesh):
    return swap(part, "zh"), swap(part, "y") if mesh.shape["y"] == 2 else part


def rows_last(far, mesh):
    return swap(far, "y") if mesh.shape["y"] == 2 else far


def rows_pieces(part, far, side, last, mesh):
    if mesh.shape["y"] == 2:
        return part, far, side, last
    value = in_order(part, far, lax.axis_index("zh"), 1)
    return (lax.all_gather(value, "y", axis=3).reshape(-1, part.shape[-1]),)


def zh_halves(value):
    place = lax.axis_index("zh")
    return pick(value, place, 2).astype(F32), pick(value, 1 - place, 2).astype(BF16)


def to_owner(summed):
    value = summed.astype(BF16).reshape((8,) + summed.shape[3:])
    return lax.all_to_all(value, ("x", "c", "zl"), 0, 0, tiled=True)


def y_swap(send, mesh):
    if mesh.shape["y"] != 2:
        return lax.psum_scatter(send, "y", scatter_dimension=1)
    return swap(send, "y")


def y_finish(keep, other, mesh):
    if mesh.shape["y"] == 2:
        other = keep.astype(F32) + other.astype(F32)
    place = lax.axis_index("zh")
    return pick(other, place, 0).astype(F32) + swap(
        pick(other, 1 - place, 0).astype(BF16), "zh"
    ).astype(F32)


def spread(value, devices):
    return lax.all_to_all(
        jnp.broadcast_to(value[None], (devices,) + value.shape), ALL, 0, 0, tiled=True
    )


def params(**kind):
    return pltpu.CompilerParams(vmem_limit_bytes=56 * MIB, **kind)


def cost(units):
    return pl.CostEstimate(flops=int(units * SCALE * 1e9), bytes_accessed=0, transcendentals=0)


HBM = pl.BlockSpec(memory_space=pl.ANY)
SCALARS = pl.BlockSpec(memory_space=pltpu.SMEM)


def load_rows(place, pieces, out, sems):
    if len(pieces) == 1:
        copies = [pltpu.make_async_copy(pieces[0], out, sems.at[0])]
    else:
        xc, zl, rows, _ = pieces[0].shape
        copies = []
        for i, piece in enumerate(pieces):
            zh, y = place[0] ^ (i % 2), place[1] ^ (i // 2)
            for j in range(xc):
                for k in range(zl):
                    row = (((j * 2 + zh) * zl + k) * 2 + y) * rows
                    row = pl.ds(pl.multiple_of(row, rows), rows)
                    copies.append(
                        pltpu.make_async_copy(
                            piece.at[j, k], out.at[row, :], sems.at[len(copies)]
                        )
                    )
    for copy in copies:
        copy.start()
    return copies


def weight_specs(*weights):
    return [HBM for weight in weights for _ in weight]


def weight_scratch(*weights):
    shapes = []
    for weight in weights:
        n = weight[0].shape[-1]
        rows = sum(piece.size for piece in weight) // n
        shapes += [pltpu.VMEM((rows, n), BF16), pltpu.SemaphoreType.DMA((32,))]
    return shapes


def own_place():
    return jnp.stack([lax.axis_index("zh"), lax.axis_index("y")]).astype(jnp.int32)


def at_first(refs, place, counts, scratch):
    @pl.when(pl.program_id(0) == 0)
    def _():
        copies, first = [], 0
        for i, count in enumerate(counts):
            copies += load_rows(place, refs[first : first + count], *scratch[2 * i : 2 * i + 2])
            first += count
        for copy in copies:
            copy.wait()


GELU_A = 0.7978845608028654
GELU_B = 0.044715
CHUNK = 256


def up_kernel(place, normed, bias, *refs):
    count = len(refs) - 4
    pieces, (pre, hidden, weight, sems) = refs[:count], refs[count:]
    at_first(pieces, place, (count,), (weight, sems))
    for first in range(0, weight.shape[1], CHUNK):
        part = slice(first, first + CHUNK)
        value = dot(normed[...], weight[:, part], 1, 0) + bias[:, part]
        pre[:, part] = value
        inner = jnp.tanh(GELU_A * (value + GELU_B * (value * value * value)))
        hidden[:, part] = (0.5 * value * (1.0 + inner)).astype(BF16)


def up_forward(normed, bias, weight, block):
    count, width = normed.shape
    n = weight[0].shape[-1]
    return pl.pallas_call(
        up_kernel,
        grid=(count // block,),
        in_specs=[
            SCALARS,
            pl.BlockSpec((block, width), lambda i: (i, 0)),
            pl.BlockSpec((1, n), lambda i: (0, 0)),
        ]
        + weight_specs(weight),
        out_specs=[pl.BlockSpec((block, n), lambda i: (i, 0))] * 2,
        out_shape=[jax.ShapeDtypeStruct((count, n), F32), jax.ShapeDtypeStruct((count, n), BF16)],
        scratch_shapes=weight_scratch(weight),
        compiler_params=params(),
        cost_estimate=cost(17),
    )(own_place(), normed, bias, *weight)


def hidden_grad_kernel(place, grad, pre, *refs):
    count = len(refs) - 4
    pieces, (out, total, weight, sems) = refs[:count], refs[count:]
    at_first(pieces, place, (count,), (weight, sems))

    @pl.when(pl.program_id(0) == 0)
    def _():
        total[...] = jnp.zeros_like(total)

    for first in range(0, weight.shape[1], CHUNK):
        part = slice(first, first + CHUNK)
        value = pre[:, part]
        square = value * value
        inner = jnp.tanh(GELU_A * (value + GELU_B * (square * value)))
        slope = 0.5 * (1.0 + inner) + 0.5 * value * (1.0 - inner * inner) * (
            GELU_A * (1.0 + 3.0 * GELU_B * square)
        )
        low = (dot(grad[...], weight[:, part], 1, 0) * slope).astype(BF16)
        out[:, part] = low
        total[:, part] += jnp.sum(low.astype(F32), 0, keepdims=True)


def hidden_backward(grad, pre, weight, block):
    count, width = grad.shape
    n = weight[0].shape[-1]
    return pl.pallas_call(
        hidden_grad_kernel,
        grid=(count // block,),
        in_specs=[
            SCALARS,
            pl.BlockSpec((block, width), lambda i: (i, 0)),
            pl.BlockSpec((block, n), lambda i: (i, 0)),
        ]
        + weight_specs(weight),
        out_specs=[
            pl.BlockSpec((block, n), lambda i: (i, 0)),
            pl.BlockSpec((1, n), lambda i: (0, 0)),
        ],
        out_shape=[jax.ShapeDtypeStruct((count, n), BF16), jax.ShapeDtypeStruct((1, n), F32)],
        scratch_shapes=weight_scratch(weight),
        compiler_params=params(),
        cost_estimate=cost(20),
    )(own_place(), grad, pre, *weight)


def weight_grad_kernel(place, left, right, keep, send):
    xc, zh, zl, rows, n = keep.shape
    value = dot(left[...], right[...], 0, 0).astype(BF16).reshape(zl, 2, rows, n)
    own = place[1] == 0
    keep[0, 0] = jnp.where(own, value[:, 0], value[:, 1])
    send[0, 0] = jnp.where(own, value[:, 1], value[:, 0])


def weight_grad_plain_kernel(left, right, out):
    out[...] = dot(left[...], right[...], 0, 0).astype(BF16)


def weight_grad(left, right, mesh):
    count, width = left.shape
    n = right.shape[1]
    y = mesh.shape["y"]
    rows = width // (16 * y)
    block = width // 8
    specs = [
        pl.BlockSpec((count, block), lambda i: (0, i)),
        pl.BlockSpec((count, n), lambda i: (0, 0), pipeline_mode=pl.Buffered(1)),
    ]
    if y != 2:
        full = pl.pallas_call(
            weight_grad_plain_kernel,
            grid=(8,),
            in_specs=specs,
            out_specs=pl.BlockSpec((block, n), lambda i: (i, 0)),
            out_shape=jax.ShapeDtypeStruct((width, n), BF16),
            compiler_params=params(),
            cost_estimate=cost(14 * n / 1024),
        )(left, right)
        return full, full
    out = pl.BlockSpec((1, 1, 2, rows, n), lambda i: (i // 2, i % 2, 0, 0, 0))
    shape = jax.ShapeDtypeStruct((4, 2, 2, rows, n), BF16)
    keep, send = pl.pallas_call(
        weight_grad_kernel,
        grid=(8,),
        in_specs=[SCALARS] + specs,
        out_specs=[out, out],
        out_shape=[shape, shape],
        compiler_params=params(),
        cost_estimate=cost(14 * n / 1024),
    )(own_place(), left, right)

    return keep, send


def sum_first(send, mesh):
    if mesh.shape["y"] == 2:
        return swap(send, "y")
    y, n = mesh.shape["y"], send.shape[-1]
    rows = send.shape[0] // (16 * y)
    return lax.psum_scatter(send.reshape(2, 2, 2, 2, y, rows, n), "y", scatter_dimension=4)


def sum_halves(keep, other, mesh):
    if mesh.shape["y"] != 2:
        return zh_halves(other)
    value = keep.astype(F32) + other.astype(F32)
    return zh_halves(value.reshape((2, 2, 2, 2) + value.shape[3:]))


def output_grad_kernel(place, left, right, keep, send):
    zh, rows, n = keep.shape
    value = dot(left[...], right[...], 0, 0).astype(BF16).reshape(zh, 2, rows, n)
    own = place[1] == 0
    keep[...] = jnp.where(own, value[:, 0], value[:, 1])
    send[...] = jnp.where(own, value[:, 1], value[:, 0])


def output_grad(left, right, mesh):
    count, wide = left.shape
    width = right.shape[1]
    y = mesh.shape["y"]
    rows = wide // (2 * y)
    if y != 2:
        full = dot(left, right, 0, 0).astype(BF16).reshape(2, y, rows, width)
        return full, full
    block = width // 4
    out = pl.BlockSpec((2, rows, block), lambda i: (0, 0, i))
    return pl.pallas_call(
        output_grad_kernel,
        grid=(4,),
        in_specs=[
            SCALARS,
            pl.BlockSpec((count, wide), lambda i: (0, 0), pipeline_mode=pl.Buffered(1)),
            pl.BlockSpec((count, block), lambda i: (0, i)),
        ],
        out_specs=[out, out],
        out_shape=[jax.ShapeDtypeStruct((2, rows, width), BF16)] * 2,
        compiler_params=params(),
        cost_estimate=cost(5),
    )(own_place(), left, right)


def joint_kernel(place, normed, bias, cosine, sine, *refs):
    count = len(refs) - 3
    pieces, (out, weight, sems) = refs[:count], refs[count:]
    at_first(pieces, place, (count,), (weight, sems))
    value = dot(normed[...], weight[...], 1, 0) + bias[...]
    third = value.shape[1] // 3
    lane = lax.broadcasted_iota(jnp.int32, (value.shape[0], PAIR), 1) % HD
    for first in range(0, 2 * third, PAIR):
        piece = turn(value[:, first : first + PAIR], cosine[...], sine[...], lane, 1.0).astype(BF16)
        if first < third:
            piece = piece * jnp.asarray(HD ** (-0.5), BF16)
        out[:, first : first + PAIR] = piece
    out[:, 2 * third :] = value[:, 2 * third :].astype(BF16)


def joint_forward(normed, bias, cosine, sine, weight, block):
    count, width = normed.shape
    n = weight[0].shape[-1]
    return pl.pallas_call(
        joint_kernel,
        grid=(count // block,),
        in_specs=[
            SCALARS,
            pl.BlockSpec((block, width), lambda i: (i, 0)),
            pl.BlockSpec((1, n), lambda i: (0, 0)),
            pl.BlockSpec((block, PAIR), lambda i: (i, 0)),
            pl.BlockSpec((block, PAIR), lambda i: (i, 0)),
        ]
        + weight_specs(weight),
        out_specs=pl.BlockSpec((block, n), lambda i: (i, 0)),
        out_shape=jax.ShapeDtypeStruct((count, n), BF16),
        scratch_shapes=weight_scratch(weight),
        compiler_params=params(),
        cost_estimate=cost(13.5),
    )(own_place(), normed, bias, cosine, sine, *weight)


def pair_kernel(dims, counts, place, one, two, *refs):
    total = sum(counts)
    pieces, (keep, send), scratch = refs[:total], refs[total : total + 2], refs[total + 2 :]
    at_first(pieces, place, counts, scratch)

    def step(out):
        for first in range(0, out.shape[1], 2 * CHUNK):
            part = slice(first, first + 2 * CHUNK)
            value = 0.0
            for left, right, dim in zip((one, two), (scratch[0], scratch[2]), dims):
                right = right[part, :] if dim == 1 else right[:, part]
                value = value + dot(left[...], right, 1, dim)
            out[:, part] = value.astype(BF16)

    half = pl.num_programs(0) // 2
    pl.when(pl.program_id(0) < half)(lambda: step(keep))
    pl.when(pl.program_id(0) >= half)(lambda: step(send))


def pair_product(one, first, two, second, dims, block, units):
    count = one.shape[0]
    width = first[0].shape[-1] if dims[0] == 0 else sum(p.size for p in first) // first[0].shape[-1]
    steps = count // block
    shape = jax.ShapeDtypeStruct((count // 2, width), BF16)
    return pl.pallas_call(
        functools.partial(pair_kernel, dims, (len(first), len(second))),
        grid=(steps,),
        in_specs=[
            SCALARS,
            pl.BlockSpec((block, one.shape[1]), lambda i: (i, 0)),
            pl.BlockSpec((block, two.shape[1]), lambda i: (i, 0)),
        ]
        + weight_specs(first, second),
        out_specs=[
            pl.BlockSpec((block, width), lambda i: (jnp.minimum(i, steps // 2 - 1), 0)),
            pl.BlockSpec((block, width), lambda i: (jnp.maximum(i - steps // 2, 0), 0)),
        ],
        out_shape=[shape, shape],
        scratch_shapes=weight_scratch(first, second),
        compiler_params=params(),
        cost_estimate=cost(units),
    )(own_place(), one, two, *first, *second)


def norm_kernel(*refs):
    blocks, (gain_ref, shift_ref, out_ref) = refs[:8], refs[8:]

    def one(ref):
        wide = ref[...].astype(F32)
        centered = wide - jnp.mean(wide, 1, keepdims=True)
        inv_std = lax.rsqrt(jnp.mean(centered * centered, 1, keepdims=True) + NORM_EPS)
        out_ref[...] = (centered * inv_std * gain_ref[...] + shift_ref[...]).astype(BF16)

    for i, ref in enumerate(blocks):
        pl.when(pl.program_id(0) == i)(functools.partial(one, ref))


def grad_kernel(*refs):
    blocks, (weight_ref, out_ref, attended_ref) = refs[:8], refs[8:]

    def one(ref):
        out_ref[...] = ref[...]
        attended_ref[...] = dot(ref[...], weight_ref[...], 1, 1).astype(BF16)

    for i, ref in enumerate(blocks):
        pl.when(pl.program_id(0) == i)(functools.partial(one, ref))


def rows_of_team(kernel, blocks, rest, widths):
    rows = blocks[0].shape[0]
    return pl.pallas_call(
        kernel,
        grid=(8,),
        in_specs=[
            pl.BlockSpec(value.shape, lambda i: (0, 0), pipeline_mode=pl.Buffered(1))
            for value in (*blocks, *rest)
        ],
        out_specs=[pl.BlockSpec((rows, wide), lambda i: (i, 0)) for wide in widths],
        out_shape=[jax.ShapeDtypeStruct((8 * rows, wide), BF16) for wide in widths],
        compiler_params=params(),
        cost_estimate=cost(11),
    )(*blocks, *rest)


def split_kernel(up, down, joint, out):
    n = up.shape[1] // 8
    for i in range(8):
        out[i, :, :n] = up[:, i * n : (i + 1) * n]
        out[i, :, n : 2 * n] = down[:, i * n : (i + 1) * n]
    for place, own, whole in head_places():
        out[place, :, 2 * n + own : 2 * n + own + PAIR] = joint[:, whole : whole + PAIR]


def join_kernel(value, out):
    n = value.shape[2]
    for i in range(8):
        out[:, i * n : (i + 1) * n] = value[i].astype(F32)


def by_columns(up, down, joint):
    rows = up.shape[0]
    wide = (up.shape[1] + down.shape[1] + joint.shape[1]) // 8
    return pl.pallas_call(
        split_kernel,
        out_shape=jax.ShapeDtypeStruct((8, rows, wide), up.dtype),
        compiler_params=params(),
        cost_estimate=cost(4),
    )(up, down, joint)


def from_columns(value):
    _, rows, n = value.shape
    return pl.pallas_call(
        join_kernel,
        out_shape=jax.ShapeDtypeStruct((rows, 8 * n), F32),
        cost_estimate=cost(3),
    )(value)


def head_places():
    for third in range(3):
        for x in range(2):
            for c in range(2):
                for zh in range(2):
                    for zl in range(2):
                        pair = ((x * 2 + c) * 2 + zh) * 2 + zl
                        yield (x * 2 + c) * 2 + zl, (third * 2 + zh) * PAIR, (third * 16 + pair) * PAIR


def join_heads_kernel(value, out):
    for place, own, whole in head_places():
        out[:, whole : whole + PAIR] = value[place, :, own : own + PAIR].astype(F32)


def from_heads(value):
    _, rows, n = value.shape
    return pl.pallas_call(
        join_heads_kernel,
        out_shape=jax.ShapeDtypeStruct((rows, 8 * n), F32),
        cost_estimate=cost(3),
    )(value)


def rows_sorted(pieces, mesh):
    if len(pieces) == 1:
        return pieces[0]
    zh, y = lax.axis_index("zh"), lax.axis_index("y")
    n = pieces[0].shape[-1]
    near = in_order(pieces[0], pieces[1], zh, 1)
    side = in_order(pieces[2], pieces[3], zh, 1)
    return in_order(near, side, y, 3).reshape(-1, n)


def turn(value, cosine, sine, lane, sign):
    half = ROT // 2
    width = value.shape[-1]
    up = pltpu.roll(value, width - half, 1)
    down = pltpu.roll(value, half, 1)
    turned = jnp.where(lane < half, -up, down)
    return value * cosine + (sign * turned) * sine


def attend_kernel(
    order, q_ref, k_ref, v_ref, do_ref, cos_ref, sin_ref, segc_ref, segr_ref,
    out_ref, grad_ref, qs, ks, vs, ds, kt, vt, segc, segr, dq, dk, dv,
):
    rows = q_ref.shape[2]
    blocks = q_ref.shape[0]
    pair = pl.program_id(1)
    scale = HD ** (-0.5)
    lane = lax.broadcasted_iota(jnp.int32, (rows, PAIR), 1) % HD

    def place(block):
        return pl.ds(pl.multiple_of(order[block] * rows, rows), rows)

    for block in range(blocks):
        at = place(block)
        qs[at, :] = q_ref[block, 0]
        ks[at, :] = k_ref[block, 0]
        kt[:, at] = k_ref[block, 0].T
        vs[at, :] = v_ref[block, 0]
        vt[:, at] = v_ref[block, 0].T
        ds[at, :] = do_ref[block, 0]
        segc[at, :] = segc_ref[block, 0]
        segr[:, at] = segr_ref[block, 0]
    dk[...] = jnp.zeros_like(dk)
    dv[...] = jnp.zeros_like(dv)
    side = lax.broadcasted_iota(jnp.int32, (rows, PAIR), 1) // HD
    causal = lax.broadcasted_iota(jnp.int32, (rows, rows), 0) <= lax.broadcasted_iota(
        jnp.int32, (rows, rows), 1
    )
    for block in range(blocks):
        here = slice(block * rows, (block + 1) * rows)
        count = (block + 1) * rows
        same = segc[:count, :1] == segr[:1, here]
        if block == 0:
            allowed = same & causal
        else:
            allowed = jnp.concatenate([same[: count - rows], same[count - rows :] & causal], 0)
        query, grad = qs[here, :], ds[here, :]
        tops = []
        turns = []
        for head in range(2):
            lanes = slice(head * HD, (head + 1) * HD)
            query_one = jnp.where(side == head, query, jnp.zeros_like(query))
            grad_one = jnp.where(side == head, grad, jnp.zeros_like(grad))
            scores = dot(ks[:count, :], query_one, 1, 1)
            scores = jnp.where(allowed, scores, NEG_FILL)
            exps = jnp.exp(scores - jnp.max(scores, 0, keepdims=True))
            probs = exps * (1.0 / jnp.sum(exps, 0, keepdims=True))
            probs_low = probs.astype(BF16)
            tops.append(dot(vt[lanes, :count], probs_low, 1, 0))
            dv[:count, :] += dot(probs_low, grad_one, 1, 0)
            probs_grad = dot(vs[:count, :], grad_one, 1, 1)
            inner = jnp.sum(probs * probs_grad, 0, keepdims=True)
            score_grad = (probs * (probs_grad - inner)).astype(BF16)
            dk[:count, :] += dot(score_grad, query_one, 1, 0)
            turns.append(dot(kt[lanes, :count], score_grad, 1, 0))
        ds[here, :] = jnp.concatenate(tops, 0).T.astype(BF16)
        dq[here, :] = (jnp.concatenate(turns, 0) * scale).T
    for block in range(blocks):
        at = place(block)
        cosine, sine = cos_ref[block, 0], sin_ref[block, 0]
        out_ref[block, 0] = ds[at, :]
        for part, source in enumerate((dq, dk)):
            spot = pl.ds(pl.multiple_of(part * 2 * PAIR + pair * PAIR, PAIR), PAIR)
            grad_ref[block, 0, :, spot] = turn(source[at, :], cosine, sine, lane, -1.0).astype(BF16)
        spot = pl.ds(pl.multiple_of(4 * PAIR + pair * PAIR, PAIR), PAIR)
        grad_ref[block, 0, :, spot] = dv[at, :].astype(BF16)


def attend(order, joint, grad, cosine, sine, segc, segr):
    blocks, seqs, rows, width = joint.shape
    span = blocks * rows
    third = width // 3

    def part(first):
        return pl.BlockSpec((blocks, 1, rows, PAIR), lambda s, p, o: (0, s, 0, first + p))

    def table(height, wide):
        return pl.BlockSpec((blocks, 1, height, wide), lambda s, p, o: (0, s, 0, 0))

    return pl.pallas_call(
        attend_kernel,
        grid_spec=pltpu.PrefetchScalarGridSpec(
            num_scalar_prefetch=1,
            grid=(seqs, third // PAIR),
            in_specs=[
                part(0),
                part(third // PAIR),
                part(2 * third // PAIR),
                part(0),
                table(rows, PAIR),
                table(rows, PAIR),
                table(rows, PAIR),
                table(8, rows),
            ],
            out_specs=[part(0), table(rows, width)],
            scratch_shapes=[
                pltpu.VMEM((span, PAIR), BF16),
                pltpu.VMEM((span, PAIR), BF16),
                pltpu.VMEM((span, PAIR), BF16),
                pltpu.VMEM((span, PAIR), BF16),
                pltpu.VMEM((PAIR, span), BF16),
                pltpu.VMEM((PAIR, span), BF16),
                pltpu.VMEM((span, PAIR), jnp.int32),
                pltpu.VMEM((8, span), jnp.int32),
                pltpu.VMEM((span, PAIR), F32),
                pltpu.VMEM((span, PAIR), F32),
                pltpu.VMEM((span, PAIR), F32),
            ],
        ),
        out_shape=[
            jax.ShapeDtypeStruct((blocks, seqs, rows, third), BF16),
            jax.ShapeDtypeStruct((blocks, seqs, rows, width), BF16),
        ],
        compiler_params=params(),
        cost_estimate=cost(33),
    )(order, joint, joint, joint, grad, cosine, sine, segc, segr)


def body(
    mesh,
    tokens,
    joint_weight,
    output_weight,
    up_weight,
    down_weight,
    joint_bias,
    output_bias,
    up_bias,
    down_bias,
    norm_gain,
    norm_shift,
    segments,
    positions,
    cotangent,
):
    rows, width = tokens.shape[1], tokens.shape[2]
    hidden_width = up_weight.shape[1]
    own_rows = joint_weight.shape[0]
    devices = mesh.size
    ix, ic, izl = (lax.axis_index(axis) for axis in ("x", "c", "zl"))
    count = 8 * rows
    heads_wide = width // 8
    units = hidden_width // 8
    own_tokens = tokens.reshape(rows, width)
    own_grad = cotangent.reshape(rows, width)

    sizes = [v.shape[0] for v in (joint_bias, up_bias, output_bias, down_bias, norm_gain, norm_shift)]
    cuts = [sum(sizes[:i]) for i in range(len(sizes) + 1)]
    small = jnp.concatenate(
        [
            value.astype(F32)
            for value in (joint_bias, up_bias, output_bias, down_bias, norm_gain, norm_shift)
        ]
        + [segments.reshape(rows).astype(F32), positions.reshape(rows).astype(F32)]
    )
    lines = -(-small.shape[0] // 128)
    small = jnp.pad(small, (0, lines * 128 - small.shape[0])).reshape(lines, 128)
    block = 2 * rows
    output_part = output_weight.reshape(1, 1, own_rows, width)
    parts = exchange(by_columns(up_weight, down_weight, joint_weight))
    output_far, output_side = rows_first(output_part, mesh)
    parts, output_far, output_side, token, small = fence(
        parts, output_far, output_side, own_tokens, small
    )
    up_part = parts[..., :units]

    up_far, up_side = rows_first(up_part, mesh)
    token_near, token_far = swap(token, "zl"), swap(token, "x")
    grad_far = swap(own_grad, "x")
    small = spread(small, devices)
    down_part, joint_part = parts[..., units : 2 * units], parts[..., 2 * units :]
    up_far, up_side, token_near, token_far, grad_far, grad, down_part, joint_part, small = fence(
        up_far, up_side, token_near, token_far, grad_far, own_grad, down_part, joint_part, small
    )

    down_far, down_side = rows_first(down_part, mesh)
    up_last = rows_last(up_far, mesh)
    token_last = swap(token_near, "x")
    grad_near = swap(grad, "zl")
    small = small.reshape(devices, lines * 128)
    joint_full, up_full, output_full, down_full, gain_full, shift_full = (
        small[:, cuts[i] : cuts[i + 1]].reshape(-1) for i in range(6)
    )
    marks = small[:, cuts[6] : cuts[6] + 2 * rows].reshape(2, 2, 2, 2, mesh.shape["y"], 2, rows)
    marks = pick(pick(marks, lax.axis_index("zh"), 2), lax.axis_index("y"), 3)
    marks = flip(flip(flip(marks, ix, 0), ic, 1), izl, 2)
    marks = marks.transpose(1, 0, 2, 3, 4).reshape(4, 2, 2, rows)
    joint_bias_mine = pick(
        pick(pick(joint_full.reshape(3, 2, 2, 2, 2, PAIR), ix, 1), ic, 1), izl, 2
    ).reshape(1, 3 * heads_wide)
    up_bias_mine = pick(up_full.reshape(8, 1, units), (ix * 2 + ic) * 2 + izl, 0)
    gain_row, shift_row = gain_full.reshape(1, width), shift_full.reshape(1, width)
    seg, pos = marks[:, :, 0].astype(jnp.int32), marks[:, :, 1]
    frequency = 10000.0 ** (-jnp.arange(0, ROT, 2, dtype=F32) / ROT)
    angles = pos[..., None] * frequency
    angles = jnp.concatenate([angles, angles], -1)
    rest = angles.shape[:-1] + (HD - ROT,)
    cosine = jnp.concatenate([jnp.cos(angles), jnp.ones(rest, F32)] * 2, -1)
    sine = jnp.concatenate([jnp.sin(angles), jnp.zeros(rest, F32)] * 2, -1)
    segc = jnp.broadcast_to(seg[..., None], seg.shape + (PAIR,))
    segr = jnp.broadcast_to(seg[:, :, None], (4, 2, 8, rows))
    rel = jnp.arange(4, dtype=jnp.int32)
    order = (2 * ((rel % 2) ^ ix) + ((rel // 2) ^ ic)).astype(jnp.int32)
    (
        down_far, down_side, up_last, token_last, joint_part, grad_near,
        cosine, sine, segc, segr, output_far, gain_row, shift_row, up_bias_mine,
    ) = fence(
        down_far, down_side, up_last, token_last, joint_part, grad_near,
        cosine, sine, segc, segr, output_far, gain_row, shift_row, up_bias_mine,
    )
    tokens = (token, token_near, token_far, token_last)
    tokens += tuple(swap(v, "c") for v in tokens)
    tokens, down_far, joint_part, grad, grad_near, output_far = fence(
        tokens, down_far, joint_part, grad, grad_near, output_far
    )

    joint_far, joint_side = rows_first(joint_part, mesh)
    down_last = rows_last(down_far, mesh)
    grad_last = swap(grad_near, "x")
    output_last = rows_last(output_far, mesh)
    (normed,) = rows_of_team(norm_kernel, tokens, (gain_row, shift_row), (width,))
    up_mine = rows_pieces(up_part, up_far, up_side, up_last, mesh)
    up_pre, hidden_low = up_forward(normed, up_bias_mine, up_mine, block)
    joint_far, joint_side, down_last, grad_last, output_last, hidden_low, normed = fence(
        joint_far, joint_side, down_last, grad_last, output_last, hidden_low, normed
    )
    output_mine = rows_sorted(
        rows_pieces(output_part, output_far, output_side, output_last, mesh), mesh
    )
    grads = (grad, grad_near, grad_far, grad_last)
    grads += tuple(swap(v, "c") for v in grads)
    grads, joint_far, output_mine = fence(grads, joint_far, output_mine)

    joint_last = rows_last(joint_far, mesh)
    grad_all, attended_grad = rows_of_team(
        grad_kernel,
        grads,
        (output_mine,),
        (width, heads_wide),
    )
    down_mine = rows_pieces(down_part, down_far, down_side, down_last, mesh)
    down_keep, down_send = weight_grad(grad_all, hidden_low, mesh)
    down_send, grad_all, attended_grad, joint_last = fence(
        down_send, grad_all, attended_grad, joint_last
    )

    down_other = sum_first(down_send, mesh)
    up_grad_low, up_total = hidden_backward(grad_all, up_pre, down_mine, block)
    up_keep, up_send = weight_grad(normed, up_grad_low, mesh)
    joint_mine = rows_pieces(joint_part, joint_far, joint_side, joint_last, mesh)
    joint_low = joint_forward(
        after(normed, up_send),
        joint_bias_mine,
        cosine.reshape(count, PAIR),
        sine.reshape(count, PAIR),
        joint_mine,
        block,
    )
    down_other, up_send, joint_low, up_grad_low = fence(down_other, up_send, joint_low, up_grad_low)

    up_other = sum_first(up_send, mesh)
    down_keep, down_send = sum_halves(down_keep, down_other, mesh)
    down_other = swap(down_send, "zh")
    attended_low, joint_grad_low = attend(
        order,
        joint_low.reshape(4, 2, rows, 3 * heads_wide),
        attended_grad.reshape(4, 2, rows, heads_wide),
        cosine,
        sine,
        segc,
        segr,
    )
    attended_low = attended_low.reshape(count, heads_wide)
    joint_grad_low = joint_grad_low.reshape(count, 3 * heads_wide)
    joint_keep, joint_send = weight_grad(normed, joint_grad_low, mesh)
    up_other, down_other, down_keep, attended_low, joint_grad_low, joint_send = fence(
        up_other, down_other, down_keep, attended_low, joint_grad_low, joint_send
    )

    joint_other = sum_first(joint_send, mesh)
    up_keep, up_send = sum_halves(up_keep, up_other, mesh)
    up_other = swap(up_send, "zh")
    down_moved = to_owner(down_keep + down_other.astype(F32))
    back_keep, back_send = pair_product(
        joint_grad_low, joint_mine, up_grad_low, up_mine, (1, 1), block, 24
    )
    out_keep, out_send = pair_product(
        after(hidden_low, back_send), down_mine, attended_low, (output_mine,), (1, 0), block, 19
    )
    output_keep, output_send = output_grad(after(attended_low, out_send), grad_all, mesh)
    joint_other, up_other, up_keep, down_moved, back_send, out_send, output_send = fence(
        joint_other, up_other, up_keep, down_moved, back_send, out_send, output_send
    )

    joint_keep, joint_send = sum_halves(joint_keep, joint_other, mesh)
    back_other = swap(back_send, "c")
    joint_send, back_other, out_send, output_send, up_other = fence(
        joint_send, back_other, out_send, output_send, up_other
    )
    joint_other = far_swap(joint_send)
    output_other = y_swap(output_send, mesh)
    up_moved = to_owner(up_keep + up_other.astype(F32))
    out_other = swap(out_send, "c")
    back = fold_first(back_keep, back_other)
    joint_other, joint_keep, up_moved, out_other, back, output_other = fence(
        joint_other, joint_keep, up_moved, out_other, back, output_other
    )

    joint_moved = to_owner(joint_keep + joint_other.astype(F32))
    produced = fold_second(back)
    out = fold_first(out_keep, out_other)
    output_weight_grad = y_finish(output_keep, output_other, mesh).reshape(own_rows, width)
    joint_moved, out, produced = fence(joint_moved, out, produced)
    produced = after(produced, out[1], out[3])
    layer_sum = fold_second(out)
    layer_out = (own_tokens.astype(F32) + output_full + down_full + layer_sum).astype(BF16)
    own_wide = own_tokens.astype(F32)
    own_centered = own_wide - jnp.mean(own_wide, 1, keepdims=True)
    own_inv = lax.rsqrt(jnp.mean(own_centered * own_centered, 1, keepdims=True) + NORM_EPS)
    normalized = own_centered * own_inv
    scaled = produced * gain_full
    tokens_grad = own_grad.astype(F32) + own_inv * (
        scaled
        - jnp.mean(scaled, 1, keepdims=True)
        - normalized * jnp.mean(scaled * normalized, 1, keepdims=True)
    )
    tokens_grad = tokens_grad.astype(BF16)

    down_weight_grad = from_columns(down_moved)
    joint_weight_grad = from_heads(joint_moved)
    up_weight_grad = from_columns(up_moved)
    joint_sum = jnp.sum(joint_grad_low.astype(F32), 0).reshape(3, 1, 1, 2, 1, PAIR)
    joint_sum = lax.dynamic_update_slice(
        jnp.zeros((3, 2, 2, 2, 2, PAIR), F32), joint_sum, (0, ix, ic, 0, izl, 0)
    )
    up_sum = lax.dynamic_update_slice(
        jnp.zeros((8, units), F32), up_total, ((ix * 2 + ic) * 2 + izl, 0)
    )
    sums = [
        joint_sum,
        up_sum,
        jnp.sum(own_grad.astype(F32), 0),
        jnp.sum(produced * normalized, 0),
        jnp.sum(produced, 0),
    ]
    sums = jnp.concatenate([v.reshape(devices, -1) for v in sums], 1)
    sums = lax.all_to_all(after(sums, layer_sum), ALL, 0, 0, tiled=True)
    sums = jnp.sum(sums, 0)
    joint_bias_grad = sums[: cuts[1]]
    up_bias_grad = sums[cuts[1] : cuts[2]]
    grad_total, norm_gain_grad, norm_shift_grad = (
        sums[cuts[2] + i * own_rows : cuts[2] + (i + 1) * own_rows] for i in range(3)
    )
    return (
        layer_out.reshape(1, rows, width),
        tokens_grad.reshape(1, rows, width),
        joint_weight_grad,
        output_weight_grad,
        up_weight_grad,
        down_weight_grad,
        joint_bias_grad,
        grad_total,
        up_bias_grad,
        grad_total,
        norm_gain_grad,
        norm_shift_grad,
    )


def solution(mesh):
    seq, dp = mesh.shape["seq"], mesh.shape["dp"]
    fine = Mesh(mesh.devices.reshape(2, seq // 2, 2, 2, dp // 4), ALL)
    row = P(ALL, None)
    one = P(ALL)
    dp_axes, seq_axes = ("zh", "zl", "y"), ("x", "c")
    token = P(dp_axes, seq_axes, None)
    mark = P(dp_axes, seq_axes)
    return jax.shard_map(
        functools.partial(body, fine),
        mesh=fine,
        in_specs=(token,) + (row,) * 4 + (one,) * 6 + (mark, mark, token),
        out_specs=(token, token) + (row,) * 4 + (one,) * 6,
        check_vma=False,
    )
```

```python
import functools

import jax
import jax.numpy as jnp
from jax import lax
from jax.experimental import pallas as pl
from jax.experimental.pallas import tpu as pltpu
from jax.sharding import Mesh
from jax.sharding import PartitionSpec as P

ALL = ("x", "c", "zh", "zl", "y")
H = 32
HD = 64
ROT = 32
PAIR = 2 * HD
NEG_FILL = -1e30
NORM_EPS = 1e-05
F32 = jnp.float32
BF16 = jnp.bfloat16


def dot(left, right, left_dim, right_dim):
    return lax.dot_general(
        left, right, (((left_dim,), (right_dim,)), ((), ())), preferred_element_type=F32
    )


MIB = 1024 * 1024
SCALE = 0.0


def after(value, *others):
    return lax.optimization_barrier((value,) + others)[0]


def fence(*values):
    return lax.optimization_barrier(values)


def swap(value, axis):
    return lax.ppermute(value, axis, [(0, 1), (1, 0)])


def pick(value, place, dim):
    return lax.dynamic_index_in_dim(value, place, dim, keepdims=False)


def in_order(own, other, place, dim):
    return jnp.where(
        place == 0, jnp.stack([own, other], dim), jnp.stack([other, own], dim)
    )


def flip(value, place, dim):
    return jnp.where(place == 0, value, jnp.flip(value, dim))


def exchange(value):
    _, rows, n = value.shape
    return lax.all_to_all(value, ("x", "c", "zl"), 0, 0, tiled=True).reshape(4, 2, rows, n)


def fold_first(keep, other):
    rows, half = keep.shape[0] // 4, keep.shape[1] // 2
    keep, other = (value.reshape(2, 2, rows, 2 * half) for value in (keep, other))

    def part(x, zl, columns):
        return keep[x, zl, :, columns].astype(F32) + other[x, zl, :, columns].astype(F32)

    one, two = slice(0, half), slice(half, 2 * half)
    send_one = jnp.stack([part(1, 0, one), part(1, 1, one)]).astype(BF16)
    send_two = jnp.stack([part(0, 1, two), part(1, 1, two)]).astype(BF16)
    other_one, other_two = swap(send_one, "x"), swap(send_two, "zl")
    return (
        part(0, 0, one) + other_one[0].astype(F32),
        (part(0, 1, one) + other_one[1].astype(F32)).astype(BF16),
        part(0, 0, two) + other_two[0].astype(F32),
        (part(1, 0, two) + other_two[1].astype(F32)).astype(BF16),
    )


def fold_second(parts):
    one, send_one, two, send_two = parts
    one = one + swap(send_one, "zl").astype(F32)
    two = two + swap(send_two, "x").astype(F32)
    return jnp.concatenate([one, two], 1)


def pause_kernel(value, out):
    out[...] = value[...]


def far_swap(value):
    other = swap(value, "zh")
    lead = (1,) * (value.ndim - 2)
    paused = pl.pallas_call(
        pause_kernel,
        grid=(1,),
        in_specs=[pl.BlockSpec(lead + (16, 128), lambda i: (0,) * value.ndim)],
        out_specs=pl.BlockSpec(lead + (16, 128), lambda i: (0,) * value.ndim),
        out_shape=jax.ShapeDtypeStruct(lead + (16, 128), BF16),
        cost_estimate=pl.CostEstimate(
            flops=60_000_000_000, bytes_accessed=0, transcendentals=0
        ),
    )(other)
    return after(other, paused)


def rows_first(part, mesh):
    return swap(part, "zh"), swap(part, "y") if mesh.shape["y"] == 2 else part


def rows_last(far, mesh):
    return swap(far, "y") if mesh.shape["y"] == 2 else far


def rows_pieces(part, far, side, last, mesh):
    if mesh.shape["y"] == 2:
        return part, far, side, last
    value = in_order(part, far, lax.axis_index("zh"), 1)
    return (lax.all_gather(value, "y", axis=3).reshape(-1, part.shape[-1]),)


def zh_halves(value):
    place = lax.axis_index("zh")
    return pick(value, place, 2).astype(F32), pick(value, 1 - place, 2).astype(BF16)


def to_owner(summed):
    value = summed.astype(BF16).reshape((8,) + summed.shape[3:])
    return lax.all_to_all(value, ("x", "c", "zl"), 0, 0, tiled=True)


def y_swap(send, mesh):
    if mesh.shape["y"] != 2:
        return lax.psum_scatter(send, "y", scatter_dimension=1)
    return swap(send, "y")


def y_finish(keep, other, mesh):
    if mesh.shape["y"] == 2:
        other = keep.astype(F32) + other.astype(F32)
    place = lax.axis_index("zh")
    return pick(other, place, 0).astype(F32) + swap(
        pick(other, 1 - place, 0).astype(BF16), "zh"
    ).astype(F32)


def spread(value, devices):
    return lax.all_to_all(
        jnp.broadcast_to(value[None], (devices,) + value.shape), ALL, 0, 0, tiled=True
    )


def params(**kind):
    return pltpu.CompilerParams(vmem_limit_bytes=56 * MIB, **kind)


def cost(units):
    return pl.CostEstimate(flops=int(units * SCALE * 1e9), bytes_accessed=0, transcendentals=0)


HBM = pl.BlockSpec(memory_space=pl.ANY)
SCALARS = pl.BlockSpec(memory_space=pltpu.SMEM)


def load_rows(place, pieces, out, sems):
    if len(pieces) == 1:
        copies = [pltpu.make_async_copy(pieces[0], out, sems.at[0])]
    else:
        xc, zl, rows, _ = pieces[0].shape
        copies = []
        for i, piece in enumerate(pieces):
            zh, y = place[0] ^ (i % 2), place[1] ^ (i // 2)
            for j in range(xc):
                for k in range(zl):
                    row = (((j * 2 + zh) * zl + k) * 2 + y) * rows
                    row = pl.ds(pl.multiple_of(row, rows), rows)
                    copies.append(
                        pltpu.make_async_copy(
                            piece.at[j, k], out.at[row, :], sems.at[len(copies)]
                        )
                    )
    for copy in copies:
        copy.start()
    return copies


def weight_specs(*weights):
    return [HBM for weight in weights for _ in weight]


def weight_scratch(*weights):
    shapes = []
    for weight in weights:
        n = weight[0].shape[-1]
        rows = sum(piece.size for piece in weight) // n
        shapes += [pltpu.VMEM((rows, n), BF16), pltpu.SemaphoreType.DMA((32,))]
    return shapes


def own_place():
    return jnp.stack([lax.axis_index("zh"), lax.axis_index("y")]).astype(jnp.int32)


def at_first(refs, place, counts, scratch):
    @pl.when(pl.program_id(0) == 0)
    def _():
        copies, first = [], 0
        for i, count in enumerate(counts):
            copies += load_rows(place, refs[first : first + count], *scratch[2 * i : 2 * i + 2])
            first += count
        for copy in copies:
            copy.wait()


GELU_A = 0.7978845608028654
GELU_B = 0.044715
CHUNK = 256


def up_kernel(place, normed, bias, *refs):
    count = len(refs) - 4
    pieces, (pre, hidden, weight, sems) = refs[:count], refs[count:]
    at_first(pieces, place, (count,), (weight, sems))
    for first in range(0, weight.shape[1], CHUNK):
        part = slice(first, first + CHUNK)
        value = dot(normed[...], weight[:, part], 1, 0) + bias[:, part]
        pre[:, part] = value
        inner = jnp.tanh(GELU_A * (value + GELU_B * (value * value * value)))
        hidden[:, part] = (0.5 * value * (1.0 + inner)).astype(BF16)


def up_forward(normed, bias, weight, block):
    count, width = normed.shape
    n = weight[0].shape[-1]
    return pl.pallas_call(
        up_kernel,
        grid=(count // block,),
        in_specs=[
            SCALARS,
            pl.BlockSpec((block, width), lambda i: (i, 0)),
            pl.BlockSpec((1, n), lambda i: (0, 0)),
        ]
        + weight_specs(weight),
        out_specs=[pl.BlockSpec((block, n), lambda i: (i, 0))] * 2,
        out_shape=[jax.ShapeDtypeStruct((count, n), F32), jax.ShapeDtypeStruct((count, n), BF16)],
        scratch_shapes=weight_scratch(weight),
        compiler_params=params(),
        cost_estimate=cost(17),
    )(own_place(), normed, bias, *weight)


def hidden_grad_kernel(place, grad, pre, *refs):
    count = len(refs) - 4
    pieces, (out, total, weight, sems) = refs[:count], refs[count:]
    at_first(pieces, place, (count,), (weight, sems))

    @pl.when(pl.program_id(0) == 0)
    def _():
        total[...] = jnp.zeros_like(total)

    for first in range(0, weight.shape[1], CHUNK):
        part = slice(first, first + CHUNK)
        value = pre[:, part]
        square = value * value
        inner = jnp.tanh(GELU_A * (value + GELU_B * (square * value)))
        slope = 0.5 * (1.0 + inner) + 0.5 * value * (1.0 - inner * inner) * (
            GELU_A * (1.0 + 3.0 * GELU_B * square)
        )
        low = (dot(grad[...], weight[:, part], 1, 0) * slope).astype(BF16)
        out[:, part] = low
        total[:, part] += jnp.sum(low.astype(F32), 0, keepdims=True)


def hidden_backward(grad, pre, weight, block):
    count, width = grad.shape
    n = weight[0].shape[-1]
    return pl.pallas_call(
        hidden_grad_kernel,
        grid=(count // block,),
        in_specs=[
            SCALARS,
            pl.BlockSpec((block, width), lambda i: (i, 0)),
            pl.BlockSpec((block, n), lambda i: (i, 0)),
        ]
        + weight_specs(weight),
        out_specs=[
            pl.BlockSpec((block, n), lambda i: (i, 0)),
            pl.BlockSpec((1, n), lambda i: (0, 0)),
        ],
        out_shape=[jax.ShapeDtypeStruct((count, n), BF16), jax.ShapeDtypeStruct((1, n), F32)],
        scratch_shapes=weight_scratch(weight),
        compiler_params=params(),
        cost_estimate=cost(20),
    )(own_place(), grad, pre, *weight)


def weight_grad_kernel(place, left, right, keep, send):
    xc, zh, zl, rows, n = keep.shape
    value = dot(left[...], right[...], 0, 0).astype(BF16).reshape(zl, 2, rows, n)
    own = place[1] == 0
    keep[0, 0] = jnp.where(own, value[:, 0], value[:, 1])
    send[0, 0] = jnp.where(own, value[:, 1], value[:, 0])


def weight_grad_plain_kernel(left, right, out):
    out[...] = dot(left[...], right[...], 0, 0).astype(BF16)


def weight_grad(left, right, mesh):
    count, width = left.shape
    n = right.shape[1]
    y = mesh.shape["y"]
    rows = width // (16 * y)
    block = width // 8
    specs = [
        pl.BlockSpec((count, block), lambda i: (0, i)),
        pl.BlockSpec((count, n), lambda i: (0, 0), pipeline_mode=pl.Buffered(1)),
    ]
    if y != 2:
        full = pl.pallas_call(
            weight_grad_plain_kernel,
            grid=(8,),
            in_specs=specs,
            out_specs=pl.BlockSpec((block, n), lambda i: (i, 0)),
            out_shape=jax.ShapeDtypeStruct((width, n), BF16),
            compiler_params=params(),
            cost_estimate=cost(14 * n / 1024),
        )(left, right)
        return full, full
    out = pl.BlockSpec((1, 1, 2, rows, n), lambda i: (i // 2, i % 2, 0, 0, 0))
    shape = jax.ShapeDtypeStruct((4, 2, 2, rows, n), BF16)
    keep, send = pl.pallas_call(
        weight_grad_kernel,
        grid=(8,),
        in_specs=[SCALARS] + specs,
        out_specs=[out, out],
        out_shape=[shape, shape],
        compiler_params=params(),
        cost_estimate=cost(14 * n / 1024),
    )(own_place(), left, right)

    return keep, send


def sum_first(send, mesh):
    if mesh.shape["y"] == 2:
        return swap(send, "y")
    y, n = mesh.shape["y"], send.shape[-1]
    rows = send.shape[0] // (16 * y)
    return lax.psum_scatter(send.reshape(2, 2, 2, 2, y, rows, n), "y", scatter_dimension=4)


def sum_halves(keep, other, mesh):
    if mesh.shape["y"] != 2:
        return zh_halves(other)
    value = keep.astype(F32) + other.astype(F32)
    return zh_halves(value.reshape((2, 2, 2, 2) + value.shape[3:]))


def output_grad_kernel(place, left, right, keep, send):
    zh, rows, n = keep.shape
    value = dot(left[...], right[...], 0, 0).astype(BF16).reshape(zh, 2, rows, n)
    own = place[1] == 0
    keep[...] = jnp.where(own, value[:, 0], value[:, 1])
    send[...] = jnp.where(own, value[:, 1], value[:, 0])


def output_grad(left, right, mesh):
    count, wide = left.shape
    width = right.shape[1]
    y = mesh.shape["y"]
    rows = wide // (2 * y)
    if y != 2:
        full = dot(left, right, 0, 0).astype(BF16).reshape(2, y, rows, width)
        return full, full
    block = width // 4
    out = pl.BlockSpec((2, rows, block), lambda i: (0, 0, i))
    return pl.pallas_call(
        output_grad_kernel,
        grid=(4,),
        in_specs=[
            SCALARS,
            pl.BlockSpec((count, wide), lambda i: (0, 0), pipeline_mode=pl.Buffered(1)),
            pl.BlockSpec((count, block), lambda i: (0, i)),
        ],
        out_specs=[out, out],
        out_shape=[jax.ShapeDtypeStruct((2, rows, width), BF16)] * 2,
        compiler_params=params(),
        cost_estimate=cost(5),
    )(own_place(), left, right)


def joint_kernel(place, normed, bias, cosine, sine, *refs):
    count = len(refs) - 3
    pieces, (out, weight, sems) = refs[:count], refs[count:]
    at_first(pieces, place, (count,), (weight, sems))
    value = dot(normed[...], weight[...], 1, 0) + bias[...]
    third = value.shape[1] // 3
    lane = lax.broadcasted_iota(jnp.int32, (value.shape[0], PAIR), 1) % HD
    for first in range(0, 2 * third, PAIR):
        piece = turn(value[:, first : first + PAIR], cosine[...], sine[...], lane, 1.0).astype(BF16)
        if first < third:
            piece = piece * jnp.asarray(HD ** (-0.5), BF16)
        out[:, first : first + PAIR] = piece
    out[:, 2 * third :] = value[:, 2 * third :].astype(BF16)


def joint_forward(normed, bias, cosine, sine, weight, block):
    count, width = normed.shape
    n = weight[0].shape[-1]
    return pl.pallas_call(
        joint_kernel,
        grid=(count // block,),
        in_specs=[
            SCALARS,
            pl.BlockSpec((block, width), lambda i: (i, 0)),
            pl.BlockSpec((1, n), lambda i: (0, 0)),
            pl.BlockSpec((block, PAIR), lambda i: (i, 0)),
            pl.BlockSpec((block, PAIR), lambda i: (i, 0)),
        ]
        + weight_specs(weight),
        out_specs=pl.BlockSpec((block, n), lambda i: (i, 0)),
        out_shape=jax.ShapeDtypeStruct((count, n), BF16),
        scratch_shapes=weight_scratch(weight),
        compiler_params=params(),
        cost_estimate=cost(13.5),
    )(own_place(), normed, bias, cosine, sine, *weight)


def pair_kernel(dims, counts, place, one, two, *refs):
    total = sum(counts)
    pieces, (keep, send), scratch = refs[:total], refs[total : total + 2], refs[total + 2 :]
    at_first(pieces, place, counts, scratch)

    def step(out):
        for first in range(0, out.shape[1], 2 * CHUNK):
            part = slice(first, first + 2 * CHUNK)
            value = 0.0
            for left, right, dim in zip((one, two), (scratch[0], scratch[2]), dims):
                right = right[part, :] if dim == 1 else right[:, part]
                value = value + dot(left[...], right, 1, dim)
            out[:, part] = value.astype(BF16)

    half = pl.num_programs(0) // 2
    pl.when(pl.program_id(0) < half)(lambda: step(keep))
    pl.when(pl.program_id(0) >= half)(lambda: step(send))


def pair_product(one, first, two, second, dims, block, units):
    count = one.shape[0]
    width = first[0].shape[-1] if dims[0] == 0 else sum(p.size for p in first) // first[0].shape[-1]
    steps = count // block
    shape = jax.ShapeDtypeStruct((count // 2, width), BF16)
    return pl.pallas_call(
        functools.partial(pair_kernel, dims, (len(first), len(second))),
        grid=(steps,),
        in_specs=[
            SCALARS,
            pl.BlockSpec((block, one.shape[1]), lambda i: (i, 0)),
            pl.BlockSpec((block, two.shape[1]), lambda i: (i, 0)),
        ]
        + weight_specs(first, second),
        out_specs=[
            pl.BlockSpec((block, width), lambda i: (jnp.minimum(i, steps // 2 - 1), 0)),
            pl.BlockSpec((block, width), lambda i: (jnp.maximum(i - steps // 2, 0), 0)),
        ],
        out_shape=[shape, shape],
        scratch_shapes=weight_scratch(first, second),
        compiler_params=params(),
        cost_estimate=cost(units),
    )(own_place(), one, two, *first, *second)


def norm_kernel(*refs):
    blocks, (gain_ref, shift_ref, out_ref) = refs[:8], refs[8:]

    def one(ref):
        wide = ref[...].astype(F32)
        centered = wide - jnp.mean(wide, 1, keepdims=True)
        inv_std = lax.rsqrt(jnp.mean(centered * centered, 1, keepdims=True) + NORM_EPS)
        out_ref[...] = (centered * inv_std * gain_ref[...] + shift_ref[...]).astype(BF16)

    for i, ref in enumerate(blocks):
        pl.when(pl.program_id(0) == i)(functools.partial(one, ref))


def grad_kernel(*refs):
    blocks, (weight_ref, out_ref, attended_ref) = refs[:8], refs[8:]

    def one(ref):
        out_ref[...] = ref[...]
        attended_ref[...] = dot(ref[...], weight_ref[...], 1, 1).astype(BF16)

    for i, ref in enumerate(blocks):
        pl.when(pl.program_id(0) == i)(functools.partial(one, ref))


def rows_of_team(kernel, blocks, rest, widths):
    rows = blocks[0].shape[0]
    return pl.pallas_call(
        kernel,
        grid=(8,),
        in_specs=[
            pl.BlockSpec(value.shape, lambda i: (0, 0), pipeline_mode=pl.Buffered(1))
            for value in (*blocks, *rest)
        ],
        out_specs=[pl.BlockSpec((rows, wide), lambda i: (i, 0)) for wide in widths],
        out_shape=[jax.ShapeDtypeStruct((8 * rows, wide), BF16) for wide in widths],
        compiler_params=params(),
        cost_estimate=cost(11),
    )(*blocks, *rest)


def split_kernel(up, down, joint, out):
    n = up.shape[1] // 8
    for i in range(8):
        out[i, :, :n] = up[:, i * n : (i + 1) * n]
        out[i, :, n : 2 * n] = down[:, i * n : (i + 1) * n]
    for place, own, whole in head_places():
        out[place, :, 2 * n + own : 2 * n + own + PAIR] = joint[:, whole : whole + PAIR]


def join_kernel(value, out):
    n = value.shape[2]
    for i in range(8):
        out[:, i * n : (i + 1) * n] = value[i].astype(F32)


def by_columns(up, down, joint):
    rows = up.shape[0]
    wide = (up.shape[1] + down.shape[1] + joint.shape[1]) // 8
    return pl.pallas_call(
        split_kernel,
        out_shape=jax.ShapeDtypeStruct((8, rows, wide), up.dtype),
        compiler_params=params(),
        cost_estimate=cost(4),
    )(up, down, joint)


def from_columns(value):
    _, rows, n = value.shape
    return pl.pallas_call(
        join_kernel,
        out_shape=jax.ShapeDtypeStruct((rows, 8 * n), F32),
        cost_estimate=cost(3),
    )(value)


def head_places():
    for third in range(3):
        for x in range(2):
            for c in range(2):
                for zh in range(2):
                    for zl in range(2):
                        pair = ((x * 2 + c) * 2 + zh) * 2 + zl
                        yield (x * 2 + c) * 2 + zl, (third * 2 + zh) * PAIR, (third * 16 + pair) * PAIR


def join_heads_kernel(value, out):
    for place, own, whole in head_places():
        out[:, whole : whole + PAIR] = value[place, :, own : own + PAIR].astype(F32)


def from_heads(value):
    _, rows, n = value.shape
    return pl.pallas_call(
        join_heads_kernel,
        out_shape=jax.ShapeDtypeStruct((rows, 8 * n), F32),
        cost_estimate=cost(3),
    )(value)


def rows_sorted(pieces, mesh):
    if len(pieces) == 1:
        return pieces[0]
    zh, y = lax.axis_index("zh"), lax.axis_index("y")
    n = pieces[0].shape[-1]
    near = in_order(pieces[0], pieces[1], zh, 1)
    side = in_order(pieces[2], pieces[3], zh, 1)
    return in_order(near, side, y, 3).reshape(-1, n)


def turn(value, cosine, sine, lane, sign):
    half = ROT // 2
    width = value.shape[-1]
    up = pltpu.roll(value, width - half, 1)
    down = pltpu.roll(value, half, 1)
    turned = jnp.where(lane < half, -up, down)
    return value * cosine + (sign * turned) * sine


def attend_kernel(
    order, q_ref, k_ref, v_ref, do_ref, cos_ref, sin_ref, segc_ref, segr_ref,
    out_ref, grad_ref, qs, ks, vs, ds, kt, vt, segc, segr, dq, dk, dv,
):
    rows = q_ref.shape[2]
    blocks = q_ref.shape[0]
    pair = pl.program_id(1)
    scale = HD ** (-0.5)
    lane = lax.broadcasted_iota(jnp.int32, (rows, PAIR), 1) % HD

    def place(block):
        return pl.ds(pl.multiple_of(order[block] * rows, rows), rows)

    for block in range(blocks):
        at = place(block)
        qs[at, :] = q_ref[block, 0]
        ks[at, :] = k_ref[block, 0]
        kt[:, at] = k_ref[block, 0].T
        vs[at, :] = v_ref[block, 0]
        vt[:, at] = v_ref[block, 0].T
        ds[at, :] = do_ref[block, 0]
        segc[at, :] = segc_ref[block, 0]
        segr[:, at] = segr_ref[block, 0]
    dk[...] = jnp.zeros_like(dk)
    dv[...] = jnp.zeros_like(dv)
    side = lax.broadcasted_iota(jnp.int32, (rows, PAIR), 1) // HD
    causal = lax.broadcasted_iota(jnp.int32, (rows, rows), 0) <= lax.broadcasted_iota(
        jnp.int32, (rows, rows), 1
    )
    for block in range(blocks):
        here = slice(block * rows, (block + 1) * rows)
        count = (block + 1) * rows
        same = segc[:count, :1] == segr[:1, here]
        if block == 0:
            allowed = same & causal
        else:
            allowed = jnp.concatenate([same[: count - rows], same[count - rows :] & causal], 0)
        query, grad = qs[here, :], ds[here, :]
        tops = []
        turns = []
        for head in range(2):
            lanes = slice(head * HD, (head + 1) * HD)
            query_one = jnp.where(side == head, query, jnp.zeros_like(query))
            grad_one = jnp.where(side == head, grad, jnp.zeros_like(grad))
            scores = dot(ks[:count, :], query_one, 1, 1)
            scores = jnp.where(allowed, scores, NEG_FILL)
            exps = jnp.exp(scores - jnp.max(scores, 0, keepdims=True))
            probs = exps * (1.0 / jnp.sum(exps, 0, keepdims=True))
            probs_low = probs.astype(BF16)
            tops.append(dot(vt[lanes, :count], probs_low, 1, 0))
            dv[:count, :] += dot(probs_low, grad_one, 1, 0)
            probs_grad = dot(vs[:count, :], grad_one, 1, 1)
            inner = jnp.sum(probs * probs_grad, 0, keepdims=True)
            score_grad = (probs * (probs_grad - inner)).astype(BF16)
            dk[:count, :] += dot(score_grad, query_one, 1, 0)
            turns.append(dot(kt[lanes, :count], score_grad, 1, 0))
        ds[here, :] = jnp.concatenate(tops, 0).T.astype(BF16)
        dq[here, :] = (jnp.concatenate(turns, 0) * scale).T
    for block in range(blocks):
        at = place(block)
        cosine, sine = cos_ref[block, 0], sin_ref[block, 0]
        out_ref[block, 0] = ds[at, :]
        for part, source in enumerate((dq, dk)):
            spot = pl.ds(pl.multiple_of(part * 2 * PAIR + pair * PAIR, PAIR), PAIR)
            grad_ref[block, 0, :, spot] = turn(source[at, :], cosine, sine, lane, -1.0).astype(BF16)
        spot = pl.ds(pl.multiple_of(4 * PAIR + pair * PAIR, PAIR), PAIR)
        grad_ref[block, 0, :, spot] = dv[at, :].astype(BF16)


def attend(order, joint, grad, cosine, sine, segc, segr):
    blocks, seqs, rows, width = joint.shape
    span = blocks * rows
    third = width // 3

    def part(first):
        return pl.BlockSpec((blocks, 1, rows, PAIR), lambda s, p, o: (0, s, 0, first + p))

    def table(height, wide):
        return pl.BlockSpec((blocks, 1, height, wide), lambda s, p, o: (0, s, 0, 0))

    return pl.pallas_call(
        attend_kernel,
        grid_spec=pltpu.PrefetchScalarGridSpec(
            num_scalar_prefetch=1,
            grid=(seqs, third // PAIR),
            in_specs=[
                part(0),
                part(third // PAIR),
                part(2 * third // PAIR),
                part(0),
                table(rows, PAIR),
                table(rows, PAIR),
                table(rows, PAIR),
                table(8, rows),
            ],
            out_specs=[part(0), table(rows, width)],
            scratch_shapes=[
                pltpu.VMEM((span, PAIR), BF16),
                pltpu.VMEM((span, PAIR), BF16),
                pltpu.VMEM((span, PAIR), BF16),
                pltpu.VMEM((span, PAIR), BF16),
                pltpu.VMEM((PAIR, span), BF16),
                pltpu.VMEM((PAIR, span), BF16),
                pltpu.VMEM((span, PAIR), jnp.int32),
                pltpu.VMEM((8, span), jnp.int32),
                pltpu.VMEM((span, PAIR), F32),
                pltpu.VMEM((span, PAIR), F32),
                pltpu.VMEM((span, PAIR), F32),
            ],
        ),
        out_shape=[
            jax.ShapeDtypeStruct((blocks, seqs, rows, third), BF16),
            jax.ShapeDtypeStruct((blocks, seqs, rows, width), BF16),
        ],
        compiler_params=params(),
        cost_estimate=cost(33),
    )(order, joint, joint, joint, grad, cosine, sine, segc, segr)


def body(
    mesh,
    tokens,
    joint_weight,
    output_weight,
    up_weight,
    down_weight,
    joint_bias,
    output_bias,
    up_bias,
    down_bias,
    norm_gain,
    norm_shift,
    segments,
    positions,
    cotangent,
):
    rows, width = tokens.shape[1], tokens.shape[2]
    hidden_width = up_weight.shape[1]
    own_rows = joint_weight.shape[0]
    devices = mesh.size
    ix, ic, izl = (lax.axis_index(axis) for axis in ("x", "c", "zl"))
    count = 8 * rows
    heads_wide = width // 8
    units = hidden_width // 8
    own_tokens = tokens.reshape(rows, width)
    own_grad = cotangent.reshape(rows, width)

    sizes = [v.shape[0] for v in (joint_bias, up_bias, output_bias, down_bias, norm_gain, norm_shift)]
    cuts = [sum(sizes[:i]) for i in range(len(sizes) + 1)]
    small = jnp.concatenate(
        [
            value.astype(F32)
            for value in (joint_bias, up_bias, output_bias, down_bias, norm_gain, norm_shift)
        ]
        + [segments.reshape(rows).astype(F32), positions.reshape(rows).astype(F32)]
    )
    lines = -(-small.shape[0] // 128)
    small = jnp.pad(small, (0, lines * 128 - small.shape[0])).reshape(lines, 128)
    block = 2 * rows
    output_part = output_weight.reshape(1, 1, own_rows, width)
    parts = exchange(by_columns(up_weight, down_weight, joint_weight))
    output_far, output_side = rows_first(output_part, mesh)
    parts, output_far, output_side, token, small = fence(
        parts, output_far, output_side, own_tokens, small
    )
    up_part = parts[..., :units]

    up_far, up_side = rows_first(up_part, mesh)
    token_near, token_far = swap(token, "zl"), swap(token, "x")
    grad_far = swap(own_grad, "x")
    small = spread(small, devices)
    down_part, joint_part = parts[..., units : 2 * units], parts[..., 2 * units :]
    up_far, up_side, token_near, token_far, grad_far, grad, down_part, joint_part, small = fence(
        up_far, up_side, token_near, token_far, grad_far, own_grad, down_part, joint_part, small
    )

    down_far, down_side = rows_first(down_part, mesh)
    up_last = rows_last(up_far, mesh)
    token_last = swap(token_near, "x")
    grad_near = swap(grad, "zl")
    small = small.reshape(devices, lines * 128)
    joint_full, up_full, output_full, down_full, gain_full, shift_full = (
        small[:, cuts[i] : cuts[i + 1]].reshape(-1) for i in range(6)
    )
    marks = small[:, cuts[6] : cuts[6] + 2 * rows].reshape(2, 2, 2, 2, mesh.shape["y"], 2, rows)
    marks = pick(pick(marks, lax.axis_index("zh"), 2), lax.axis_index("y"), 3)
    marks = flip(flip(flip(marks, ix, 0), ic, 1), izl, 2)
    marks = marks.transpose(1, 0, 2, 3, 4).reshape(4, 2, 2, rows)
    joint_bias_mine = pick(
        pick(pick(joint_full.reshape(3, 2, 2, 2, 2, PAIR), ix, 1), ic, 1), izl, 2
    ).reshape(1, 3 * heads_wide)
    up_bias_mine = pick(up_full.reshape(8, 1, units), (ix * 2 + ic) * 2 + izl, 0)
    gain_row, shift_row = gain_full.reshape(1, width), shift_full.reshape(1, width)
    seg, pos = marks[:, :, 0].astype(jnp.int32), marks[:, :, 1]
    frequency = 10000.0 ** (-jnp.arange(0, ROT, 2, dtype=F32) / ROT)
    angles = pos[..., None] * frequency
    angles = jnp.concatenate([angles, angles], -1)
    rest = angles.shape[:-1] + (HD - ROT,)
    cosine = jnp.concatenate([jnp.cos(angles), jnp.ones(rest, F32)] * 2, -1)
    sine = jnp.concatenate([jnp.sin(angles), jnp.zeros(rest, F32)] * 2, -1)
    segc = jnp.broadcast_to(seg[..., None], seg.shape + (PAIR,))
    segr = jnp.broadcast_to(seg[:, :, None], (4, 2, 8, rows))
    rel = jnp.arange(4, dtype=jnp.int32)
    order = (2 * ((rel % 2) ^ ix) + ((rel // 2) ^ ic)).astype(jnp.int32)
    (
        down_far, down_side, up_last, token_last, joint_part, grad_near,
        cosine, sine, segc, segr, output_far, gain_row, shift_row, up_bias_mine,
    ) = fence(
        down_far, down_side, up_last, token_last, joint_part, grad_near,
        cosine, sine, segc, segr, output_far, gain_row, shift_row, up_bias_mine,
    )
    tokens = (token, token_near, token_far, token_last)
    tokens += tuple(swap(v, "c") for v in tokens)
    tokens, down_far, joint_part, grad, grad_near, output_far = fence(
        tokens, down_far, joint_part, grad, grad_near, output_far
    )

    joint_far, joint_side = rows_first(joint_part, mesh)
    down_last = rows_last(down_far, mesh)
    grad_last = swap(grad_near, "x")
    output_last = rows_last(output_far, mesh)
    (normed,) = rows_of_team(norm_kernel, tokens, (gain_row, shift_row), (width,))
    up_mine = rows_pieces(up_part, up_far, up_side, up_last, mesh)
    up_pre, hidden_low = up_forward(normed, up_bias_mine, up_mine, block)
    joint_far, joint_side, down_last, grad_last, output_last, hidden_low, normed = fence(
        joint_far, joint_side, down_last, grad_last, output_last, hidden_low, normed
    )
    output_mine = rows_sorted(
        rows_pieces(output_part, output_far, output_side, output_last, mesh), mesh
    )
    grads = (grad, grad_near, grad_far, grad_last)
    grads += tuple(swap(v, "c") for v in grads)
    grads, joint_far, output_mine = fence(grads, joint_far, output_mine)

    joint_last = rows_last(joint_far, mesh)
    grad_all, attended_grad = rows_of_team(
        grad_kernel,
        grads,
        (output_mine,),
        (width, heads_wide),
    )
    down_mine = rows_pieces(down_part, down_far, down_side, down_last, mesh)
    down_keep, down_send = weight_grad(grad_all, hidden_low, mesh)
    down_send, grad_all, attended_grad, joint_last = fence(
        down_send, grad_all, attended_grad, joint_last
    )

    down_other = sum_first(down_send, mesh)
    up_grad_low, up_total = hidden_backward(grad_all, up_pre, down_mine, block)
    up_keep, up_send = weight_grad(normed, up_grad_low, mesh)
    joint_mine = rows_pieces(joint_part, joint_far, joint_side, joint_last, mesh)
    joint_low = joint_forward(
        after(normed, up_send),
        joint_bias_mine,
        cosine.reshape(count, PAIR),
        sine.reshape(count, PAIR),
        joint_mine,
        block,
    )
    down_other, up_send, joint_low, up_grad_low = fence(down_other, up_send, joint_low, up_grad_low)

    up_other = sum_first(up_send, mesh)
    down_keep, down_send = sum_halves(down_keep, down_other, mesh)
    down_other = swap(down_send, "zh")
    attended_low, joint_grad_low = attend(
        order,
        joint_low.reshape(4, 2, rows, 3 * heads_wide),
        attended_grad.reshape(4, 2, rows, heads_wide),
        cosine,
        sine,
        segc,
        segr,
    )
    attended_low = attended_low.reshape(count, heads_wide)
    joint_grad_low = joint_grad_low.reshape(count, 3 * heads_wide)
    joint_keep, joint_send = weight_grad(normed, joint_grad_low, mesh)
    up_other, down_other, down_keep, attended_low, joint_grad_low, joint_send = fence(
        up_other, down_other, down_keep, attended_low, joint_grad_low, joint_send
    )

    joint_other = sum_first(joint_send, mesh)
    up_keep, up_send = sum_halves(up_keep, up_other, mesh)
    up_other = swap(up_send, "zh")
    down_moved = to_owner(down_keep + down_other.astype(F32))
    back_keep, back_send = pair_product(
        joint_grad_low, joint_mine, up_grad_low, up_mine, (1, 1), block, 24
    )
    out_keep, out_send = pair_product(
        after(hidden_low, back_send), down_mine, attended_low, (output_mine,), (1, 0), block, 19
    )
    output_keep, output_send = output_grad(after(attended_low, out_send), grad_all, mesh)
    joint_other, up_other, up_keep, down_moved, back_send, out_send, output_send = fence(
        joint_other, up_other, up_keep, down_moved, back_send, out_send, output_send
    )

    joint_keep, joint_send = sum_halves(joint_keep, joint_other, mesh)
    back_other = swap(back_send, "c")
    joint_send, back_other = fence(joint_send, back_other)
    joint_other = far_swap(joint_send)
    output_other = y_swap(output_send, mesh)
    up_moved = to_owner(up_keep + up_other.astype(F32))
    out_other = swap(out_send, "c")
    back = fold_first(back_keep, back_other)
    joint_other, joint_keep, up_moved, out_other, back, output_other = fence(
        joint_other, joint_keep, up_moved, out_other, back, output_other
    )

    joint_moved = to_owner(joint_keep + joint_other.astype(F32))
    produced = fold_second(back)
    out = fold_first(out_keep, out_other)
    output_weight_grad = y_finish(output_keep, output_other, mesh).reshape(own_rows, width)
    joint_moved, out, produced = fence(joint_moved, out, produced)
    produced = after(produced, out[1], out[3])
    layer_sum = fold_second(out)
    layer_out = (own_tokens.astype(F32) + output_full + down_full + layer_sum).astype(BF16)
    own_wide = own_tokens.astype(F32)
    own_centered = own_wide - jnp.mean(own_wide, 1, keepdims=True)
    own_inv = lax.rsqrt(jnp.mean(own_centered * own_centered, 1, keepdims=True) + NORM_EPS)
    normalized = own_centered * own_inv
    scaled = produced * gain_full
    tokens_grad = own_grad.astype(F32) + own_inv * (
        scaled
        - jnp.mean(scaled, 1, keepdims=True)
        - normalized * jnp.mean(scaled * normalized, 1, keepdims=True)
    )
    tokens_grad = tokens_grad.astype(BF16)

    down_weight_grad = from_columns(down_moved)
    joint_weight_grad = from_heads(joint_moved)
    up_weight_grad = from_columns(up_moved)
    joint_sum = jnp.sum(joint_grad_low.astype(F32), 0).reshape(3, 1, 1, 2, 1, PAIR)
    joint_sum = lax.dynamic_update_slice(
        jnp.zeros((3, 2, 2, 2, 2, PAIR), F32), joint_sum, (0, ix, ic, 0, izl, 0)
    )
    up_sum = lax.dynamic_update_slice(
        jnp.zeros((8, units), F32), up_total, ((ix * 2 + ic) * 2 + izl, 0)
    )
    sums = [
        joint_sum,
        up_sum,
        jnp.sum(own_grad.astype(F32), 0),
        jnp.sum(produced * normalized, 0),
        jnp.sum(produced, 0),
    ]
    sums = jnp.concatenate([v.reshape(devices, -1) for v in sums], 1)
    sums = lax.all_to_all(after(sums, layer_sum), ALL, 0, 0, tiled=True)
    sums = jnp.sum(sums, 0)
    joint_bias_grad = sums[: cuts[1]]
    up_bias_grad = sums[cuts[1] : cuts[2]]
    grad_total, norm_gain_grad, norm_shift_grad = (
        sums[cuts[2] + i * own_rows : cuts[2] + (i + 1) * own_rows] for i in range(3)
    )
    return (
        layer_out.reshape(1, rows, width),
        tokens_grad.reshape(1, rows, width),
        joint_weight_grad,
        output_weight_grad,
        up_weight_grad,
        down_weight_grad,
        joint_bias_grad,
        grad_total,
        up_bias_grad,
        grad_total,
        norm_gain_grad,
        norm_shift_grad,
    )


def solution(mesh):
    seq, dp = mesh.shape["seq"], mesh.shape["dp"]
    fine = Mesh(mesh.devices.reshape(2, seq // 2, 2, 2, dp // 4), ALL)
    row = P(ALL, None)
    one = P(ALL)
    dp_axes, seq_axes = ("zh", "zl", "y"), ("x", "c")
    token = P(dp_axes, seq_axes, None)
    mark = P(dp_axes, seq_axes)
    return jax.shard_map(
        functools.partial(body, fine),
        mesh=fine,
        in_specs=(token,) + (row,) * 4 + (one,) * 6 + (mark, mark, token),
        out_specs=(token, token) + (row,) * 4 + (one,) * 6,
        check_vma=False,
    )
```
